32 devices in a mesh: grp: 2 (over y), row: 8 (over z, x), col: 2 (over core).
Axes of the slice: x: 2, y: 2, z: 4, core: 2. Of those that a mesh axis runs over, the one named last changes fastest.
Arguments:
- matrix: float32 [12288, 6144], P(('grp', 'row'), 'col'), parts along dimension 0, as said below
- panel: float32 [12288, 256], P(('grp', 'row')), parts along dimension 0, as said below
Outputs:
- updated: float32 [12288, 6144], P(('grp', 'row'), 'col'), parts along dimension 0
- basis: float32 [12288, 256], P(('grp', 'row')), parts along dimension 0
There are 2 independent parts, one for each index of `grp`. The reference program is written for one: setup_inputs(seed, part) draws one part's arguments, and reference() takes and returns one part's arrays. A program takes and returns all parts, laid end to end along the dimension named above; each array names one. Nothing has to cross between parts.
Inputs may be any that keep to these rules, and one draw needn't show every extreme that they name: matrix is symmetric. panel has full column rank.
All inputs are finite; a program needn't handle non-finite values.
Results may differ from the reference program's by a relative error of at most 0.000071.
Values sent between devices are 32-bit elements; how exact they have to be, the bound alone decides.
No kernel may reach another device: no remote copies, remote signals or barrier semaphores. Data moves between devices by JAX's collectives and lax.ppermute only.
A program may use at most 64 MiB of HBM per device.

```python
import jax
import jax.numpy as jnp
from jax import lax

N = 6144
B = 256


def draw_matrix(key, part):
    base = jax.random.normal(key, (N, N), jnp.float32)
    return (0.5 * (base + base.T)).astype(jnp.float32)


def draw_panel(key, part):
    position = jnp.arange(N, dtype=jnp.float32) / N
    values = jax.random.normal(jax.random.fold_in(key, 3), (N, B), jnp.float32)
    scales = jnp.exp(jnp.log(3.0) * position)
    return (values * scales[:, None]).astype(jnp.float32)


def setup_inputs(seed: int = 0, part: int = 0) -> dict:
    key_list = jax.random.split(jax.random.key(seed), 3)
    own_keys = jax.random.split(jax.random.fold_in(key_list[2], part), 3)
    return {
        "matrix": draw_matrix(jax.random.fold_in(jax.random.fold_in(key_list[2], part), 71), part),
        "panel": draw_panel(jax.random.fold_in(jax.random.fold_in(key_list[2], part), 71), part),
    }


def mult(a, b):
    return jnp.dot(a.astype(jnp.float32), b.astype(jnp.float32), preferred_element_type=jnp.float32, precision=lax.Precision.HIGHEST)

def reference(matrix, panel):
    gram = mult(panel.T, panel)
    lower = jnp.linalg.cholesky(gram)
    basis = lax.linalg.triangular_solve(lower, panel, left_side=False, lower=True, transpose_a=True)
    image = mult(matrix, basis)
    coupling = mult(basis.T, image)
    reflected = 2.0 * image - 2.0 * mult(basis, coupling)
    updated = matrix - mult(basis, reflected.T) - mult(reflected, basis.T)
    return (updated, basis)
```

```python
import jax
import jax.numpy as jnp
from jax import lax
from jax.sharding import PartitionSpec as P

WALK = (0, 2, 4, 6, 7, 5, 3, 1)
FULL = lax.Precision.HIGHEST
THREE = lax.Precision.HIGH


def dot(a, b, dims=((1,), (0,)), precision=FULL):
    return lax.dot_general(
        a, b, (dims, ((), ())), precision=precision, preferred_element_type=jnp.float32
    )


def swap(x):
    return lax.ppermute(x, "col", ((0, 1), (1, 0)))


def gather(part):
    count = lax.axis_size("row")
    if count != len(WALK):
        return lax.all_gather(part, "row", axis=0)
    ahead = tuple((WALK[i], WALK[(i + 1) % count]) for i in range(count))
    back = tuple((b, a) for a, b in ahead)
    place = [WALK.index(i) for i in range(count)]
    here = jnp.asarray(place, jnp.int32)[lax.axis_index("row")]
    walk = jnp.asarray(WALK, jnp.int32)
    height, width = part.shape
    out = jnp.zeros((count, height, width), part.dtype)

    def put(out, x, step, low=0):
        return lax.dynamic_update_slice(
            out, x[None], (walk[(here + step) % count], low, 0)
        )

    out = put(out, part, 0)
    one, two = part, part
    for step in range(1, count // 2):
        one = lax.ppermute(one, "row", ahead)
        two = lax.ppermute(two, "row", back)
        out = put(out, one, count - step)
        out = put(out, two, step)
    middle = height // 2
    one = lax.ppermute(one[:middle], "row", ahead)
    two = lax.ppermute(two[middle:], "row", back)
    out = put(out, one, count // 2)
    return put(out, two, count // 2, middle)


def columns(halves, core):
    count, height, width = halves.shape
    mine = lax.dynamic_slice_in_dim(halves, core * (count // 2), count // 2, 0)
    other = lax.dynamic_slice_in_dim(halves, (1 - core) * (count // 2), count // 2, 0)
    other = swap(other)
    first = jnp.where(core == 0, mine, other)
    second = jnp.where(core == 0, other, mine)
    return jnp.concatenate([first[:, None], second[:, None]], 1).reshape(-1, width)


def both(core, mine, other):
    return jnp.concatenate(
        [jnp.where(core == 0, mine, other), jnp.where(core == 0, other, mine)], 0
    )


def body(matrix, panel):
    core = lax.axis_index("col")
    height, width = panel.shape
    half = height // 2
    panel_half = lax.dynamic_slice_in_dim(panel, core * half, half, 0)
    panel_halves = gather(panel_half)
    flat = panel_halves.reshape(-1, width)
    gram = dot(flat, flat, ((0,), (0,)))
    gram = gram + swap(gram)
    panel_cols = columns(panel_halves, core)
    terms = dot(matrix, panel_cols, precision=THREE)
    mine = lax.dynamic_slice_in_dim(terms, core * half, half, 0)
    other = lax.dynamic_slice_in_dim(terms, (1 - core) * half, half, 0)
    image_half = mine + swap(other)
    image_halves = gather(image_half)

    lower = lax.linalg.cholesky(gram, symmetrize_input=False)
    inverse = lax.linalg.triangular_solve(
        lower, jnp.eye(width, dtype=jnp.float32), left_side=True, lower=True
    )
    basis = dot(panel, inverse, ((1,), (1,)))
    left = dot(2.0 * basis, inverse)
    image = both(core, image_half, swap(image_half))
    image = dot(image, inverse, ((1,), (1,)))

    flat_image = image_halves.reshape(-1, width)
    inner = dot(flat, flat_image, ((0,), (0,)))
    inner = inner + swap(inner)
    image_cols = columns(image_halves, core)
    coupling = dot(dot(inverse, inner), inverse, ((1,), (1,)))
    right = dot(2.0 * image - 4.0 * dot(basis, coupling), inverse)
    updated = matrix - dot(
        jnp.concatenate([left, right], 1),
        jnp.concatenate([image_cols, panel_cols], 1),
        ((1,), (1,)),
        THREE,
    )
    return (updated, basis)


def solution(mesh):
    return jax.shard_map(
        body,
        mesh=mesh,
        in_specs=(P(("grp", "row"), "col"), P(("grp", "row"), None)),
        out_specs=(P(("grp", "row"), "col"), P(("grp", "row"), None)),
        check_vma=False,
    )
```

```python
import functools

import jax
import jax.numpy as jnp
import numpy as np
from jax import lax
from jax.experimental import pallas as pl
from jax.experimental.pallas import tpu as pltpu
from jax.sharding import PartitionSpec as P

WALK = (0, 2, 4, 6, 7, 5, 3, 1)
FULL = lax.Precision.HIGHEST
THREE = lax.Precision.HIGH


def dot(a, b, dims=((1,), (0,)), precision=FULL):
    return lax.dot_general(
        a, b, (dims, ((), ())), precision=precision, preferred_element_type=jnp.float32
    )


def swap(x):
    return lax.ppermute(x, "col", ((0, 1), (1, 0)))


def gather(part):
    return lax.all_gather(part, "row", axis=0)


def columns(halves, core):
    count, height, width = halves.shape
    mine = lax.dynamic_slice_in_dim(halves, core * (count // 2), count // 2, 0)
    other = lax.dynamic_slice_in_dim(halves, (1 - core) * (count // 2), count // 2, 0)
    other = swap(other)
    first = jnp.where(core == 0, mine, other)
    second = jnp.where(core == 0, other, mine)
    return jnp.concatenate([first[:, None], second[:, None]], 1).reshape(-1, width)


def both(core, mine, other):
    return jnp.concatenate(
        [jnp.where(core == 0, mine, other), jnp.where(core == 0, other, mine)], 0
    )


def plain(matrix, panel):
    core = lax.axis_index("col")
    height, width = panel.shape
    half = height // 2
    panel_half = lax.dynamic_slice_in_dim(panel, core * half, half, 0)
    panel_halves = gather(panel_half)
    flat = panel_halves.reshape(-1, width)
    gram = dot(flat, flat, ((0,), (0,)))
    gram = gram + swap(gram)
    panel_cols = columns(panel_halves, core)
    terms = dot(matrix, panel_cols, precision=THREE)
    mine = lax.dynamic_slice_in_dim(terms, core * half, half, 0)
    other = lax.dynamic_slice_in_dim(terms, (1 - core) * half, half, 0)
    image_half = mine + swap(other)
    image_halves = gather(image_half)

    lower = lax.linalg.cholesky(gram, symmetrize_input=False)
    inverse = lax.linalg.triangular_solve(
        lower, jnp.eye(width, dtype=jnp.float32), left_side=True, lower=True
    )
    basis = dot(panel, inverse, ((1,), (1,)))
    left = dot(2.0 * basis, inverse)
    image = both(core, image_half, swap(image_half))
    image = dot(image, inverse, ((1,), (1,)))

    flat_image = image_halves.reshape(-1, width)
    inner = dot(flat, flat_image, ((0,), (0,)))
    inner = inner + swap(inner)
    image_cols = columns(image_halves, core)
    coupling = dot(dot(inverse, inner), inverse, ((1,), (1,)))
    right = dot(2.0 * image - 4.0 * dot(basis, coupling), inverse)
    updated = matrix - dot(
        jnp.concatenate([left, right], 1),
        jnp.concatenate([image_cols, panel_cols], 1),
        ((1,), (1,)),
        THREE,
    )
    return (updated, basis)


AXES = ("row", "col")
COUNT = len(WALK)


def flat(place, core):
    return WALK[place % COUNT] * 2 + core


ROUND = tuple((flat(i, 0), flat(i + 1, 0)) for i in range(COUNT)) + tuple(
    (flat(i, 1), flat(i - 1, 1)) for i in range(COUNT)
)


def order_table():
    table = np.zeros((COUNT, 2, 4, 2), np.int32)
    for row in range(COUNT):
        place = WALK.index(row)
        for core in range(2):
            away = -1 if core == 0 else 1
            found = []
            for piece in range(COUNT):
                step, first = (piece + 1) // 2, piece % 2 == 1
                origin = WALK[(place + (away if first else -away) * step) % COUNT]
                if origin // 4 == core:
                    found.append((step, piece, origin % 4))
            found.sort()
            for k, (_, piece, block) in enumerate(found):
                table[row, core, k] = piece, block
    return table.reshape(COUNT * 2, 8)


def split(x):
    high = x.astype(jnp.bfloat16)
    return high, (x - high.astype(jnp.float32)).astype(jnp.bfloat16)


def dot3(a, b, dims=((1,), (0,))):
    one = lambda x, y: lax.dot_general(
        x, y, (dims, ((), ())), preferred_element_type=jnp.float32
    )
    return one(a[0], b[0]) + (one(a[0], b[1]) + one(a[1], b[0]))


TURNED = ((0,), (0,))
ACROSS = ((1,), (1,))


def wide(pieces):
    return jnp.concatenate([x[...] for x in pieces], 1)


def cost(flops, bytes_accessed):
    return pl.CostEstimate(
        flops=int(flops), bytes_accessed=int(bytes_accessed), transcendentals=0
    )


def vmem():
    return pl.BlockSpec(memory_space=pltpu.VMEM)


def anywhere():
    return pl.BlockSpec(memory_space=pl.ANY)


PARAMS = pltpu.CompilerParams(vmem_limit_bytes=56 * 1024 * 1024)


def inner_kernel(start, count, *refs):
    total, pieces, out = refs[:start], refs[start:-1], refs[-1]
    acc = total[0][...] if start else None
    lefts, rights = pieces[:count], pieces[count:]
    rights = rights or lefts
    for i in range(0, count, 2):
        left, right = wide(lefts[i : i + 2]), wide(rights[i : i + 2])
        term = dot(left, right, TURNED)
        acc = term if acc is None else acc + term
    out[...] = acc


def inner(total, lefts, rights=()):
    width = 2 * lefts[0].shape[1]
    rows = sum(x.shape[0] for x in lefts[::2])
    args = ([] if total is None else [total]) + list(lefts) + list(rights)
    return pl.pallas_call(
        functools.partial(inner_kernel, 0 if total is None else 1, len(lefts)),
        out_shape=jax.ShapeDtypeStruct((width, width), jnp.float32),
        in_specs=[vmem()] * len(args),
        out_specs=vmem(),
        compiler_params=PARAMS,
        cost_estimate=cost(12 * rows * width * width, 8 * rows * width),
    )(*args)


def fetch(pieces, which, lands, sems):
    whole, parts = pieces
    for index, pair in enumerate(whole):
        @pl.when(which == index)
        def _():
            for side in range(2):
                pltpu.make_async_copy(pair[side], lands[side], sems.at[side]).start()

    if parts:
        half = parts[0][0].shape[0]

        @pl.when(which == COUNT - 1)
        def _():
            core = lax.axis_index("col")
            for part in range(2):
                low = pl.multiple_of(half * jnp.where(core == 0, part, 1 - part), half)
                for side in range(2):
                    pltpu.make_async_copy(
                        parts[part][side],
                        lands[side].at[pl.ds(low, half)],
                        sems.at[side],
                    ).start()


def landed(lands, sems):
    for side in range(2):
        pltpu.make_async_copy(lands[side], lands[side], sems.at[side]).wait()


def pair_up(refs):
    return [refs[i : i + 2] for i in range(0, len(refs), 2)]


def term_kernel(first, blocks, whole, parts, *refs):
    table, matrix = refs[:2]
    refs = refs[2:]
    start = 1 if first else 0
    total, refs = refs[:start], refs[start:]
    count = 2 * (whole + parts)
    pieces, (out, kept, land, other, sems) = pair_up(refs[:count]), refs[count:]
    step = pl.program_id(0)
    lands = (land, other)
    fetch((pieces[:whole], pieces[whole:]), table[2 * (first + step)], lands, sems)
    left = split(matrix[...])

    @pl.when(step == 0)
    def _():
        out[...] = total[0][...] if start else jnp.zeros_like(out)

    landed(lands, sems)
    rows = wide(lands)
    kept[...] = rows
    out[...] += dot3(left, split(rows))


def terms(table, matrix, total, pieces, first, blocks):
    height = matrix.shape[0]
    width = 2 * pieces[0][0].shape[1]
    whole = sum(x[0].shape[0] == height for x in pieces)
    flat_pieces = [x for pair in pieces for x in pair]
    block = pl.BlockSpec(
        (height, height), lambda i, table: (0, table[2 * (first + i) + 1])
    )
    fixed = pl.BlockSpec((height, width), lambda i, table: (0, 0))
    begin = [] if total is None else [total]
    return pl.pallas_call(
        functools.partial(term_kernel, first, blocks, whole, len(pieces) - whole),
        grid_spec=pltpu.PrefetchScalarGridSpec(
            num_scalar_prefetch=1,
            grid=(blocks,),
            in_specs=[block] + [fixed] * len(begin) + [anywhere()] * len(flat_pieces),
            out_specs=[fixed, pl.BlockSpec((height, width), lambda i, table: (i, 0))],
            scratch_shapes=[pltpu.VMEM((height, width // 2), jnp.float32)] * 2
            + [pltpu.SemaphoreType.DMA((2,))],
        ),
        out_shape=[
            jax.ShapeDtypeStruct((height, width), jnp.float32),
            jax.ShapeDtypeStruct((blocks * height, width), jnp.float32),
        ],
        compiler_params=PARAMS,
        cost_estimate=cost(
            6 * blocks * height * height * width, 4 * blocks * height * height
        ),
    )(table, matrix, *begin, *flat_pieces)


def factor(gram_ref, out, work, rows, block=64, group=8):
    size = gram_ref.shape[0]
    work[...] = gram_ref[...]
    line = lax.broadcasted_iota(jnp.int32, (size, size), 0)
    lane = lax.broadcasted_iota(jnp.int32, (size, size), 1)
    rows[...] = jnp.where(line == lane, 1.0, 0.0).astype(jnp.float32)
    index = lax.broadcasted_iota(jnp.int32, (block, 128), 0)
    for top in range(0, size, block):
        low = top // 128 * 128
        high = low + 128
        strip = jnp.concatenate(
            [work[top : top + block, low:], rows[top : top + block, :high]], 1
        )
        tiles = strip.shape[1] // 128
        spread = lambda x: jnp.concatenate([x] * tiles, 1)
        pivots = jnp.ones((block, 128), jnp.float32)
        for j in range(0, block, group):
            at = top - low + j
            some = range(group)
            down = [
                jnp.broadcast_to(strip[:, at + m : at + m + 1], (block, 128))
                for m in some
            ]
            along = [strip[j + m : j + m + 1, :] for m in some]
            cell = {
                (m, i): jnp.broadcast_to(
                    strip[j + m : j + m + 1, at + i : at + i + 1], (1, 128)
                )
                for m in some
                for i in range(m, group)
            }
            for m in some:
                over = 1.0 / cell[m, m]
                pivots = jnp.where(index == j + m, cell[m, m], pivots)
                row = along[m] * spread(over)
                strip = strip - spread(jnp.where(index > j + m, down[m], 0.0)) * row
                for i in range(m + 1, group):
                    ratio = cell[m, i] * over
                    along[i] = along[i] - spread(cell[m, i]) * row
                    down[i] = down[i] - down[m] * ratio
                    for h in range(i, group):
                        cell[i, h] = cell[i, h] - cell[m, h] * ratio
        strip = strip * spread(lax.rsqrt(pivots))
        out[top : top + block, :high] = strip[:, size - low :]
        if high < size:
            out[top : top + block, high:] = jnp.zeros(
                (block, size - high), jnp.float32
            )
        after = top + block
        if after < size:
            base = after // 128 * 128
            update = dot(strip[:, base - low : size - low], strip[:, base - low :], TURNED)
            update = update[after - base :]
            work[after:, base:] -= update[:, : size - base]
            rows[after:, :high] -= update[:, size - base :]


def factor_kernel(gram, out, work, rows):
    factor(gram, out, work, rows)


def inverse_factor(gram):
    size = gram.shape[0]
    return pl.pallas_call(
        factor_kernel,
        out_shape=jax.ShapeDtypeStruct((size, size), jnp.float32),
        in_specs=[vmem()],
        out_specs=vmem(),
        scratch_shapes=[pltpu.VMEM((size, size), jnp.float32)] * 2,
        compiler_params=PARAMS,
        cost_estimate=cost(10e-6 * 1e15, 4 * size * size),
    )(gram)


def left_kernel(panel, image0, image1, inverse, basis, left, right):
    inv = inverse[...]
    rows = dot(panel[...], inv, ACROSS)
    basis[...] = rows
    left[...] = dot(2.0 * rows, inv)
    right[...] = dot(2.0 * dot(wide((image0, image1)), inv, ACROSS), inv)


def lefts(panel, images, inverse):
    height, width = panel.shape
    return pl.pallas_call(
        left_kernel,
        out_shape=[jax.ShapeDtypeStruct((height, width), jnp.float32)] * 3,
        in_specs=[vmem()] * 4,
        out_specs=[vmem()] * 3,
        compiler_params=PARAMS,
        cost_estimate=cost(48 * height * width * width, 20 * height * width),
    )(panel, *images, inverse)


def update_kernel(blocks, *refs):
    table, matrix, kept0, kept1, kept2, total, inverse, basis, left, right = refs[:10]
    pieces, (lasts) = pair_up(refs[10 : 10 + 2 * (COUNT + 1)]), refs[28:32]
    out, one, two, three, four, land, other, sems = refs[32:]
    step = pl.program_id(0)
    width = basis.shape[1]
    slots = lambda k: (land.at[k], other.at[k])

    @pl.when(step == 0)
    def _():
        for k in range(blocks):
            fetch((pieces[:7], pieces[7:]), table[2 * k], slots(k), sems.at[k])
        acc = total[...]
        acc += dot(wide(lasts[:2]), wide(pieces[7]), TURNED)
        acc += dot(wide(lasts[2:]), wide(pieces[8]), TURNED)
        inv = inverse[...]
        coupling = dot(dot(inv, acc), inv, ACROSS)
        y = right[...] - dot(basis[...], dot(4.0 * coupling, inv))
        one[...], two[...] = split(left[...])
        three[...], four[...] = split(y)

    kept = jnp.where(step == 0, kept0[...], jnp.where(step == 3, kept2[...], kept1[...]))
    lands = (land.at[step], other.at[step])
    landed(lands, sems.at[step])
    part = dot3((three[...], four[...]), split(kept), ACROSS)
    part += dot3((one[...], two[...]), split(wide(lands)), ACROSS)
    out[...] = matrix[...] - part


def update(table, matrix, kept, total, inverse, basis, left, right, pieces, lasts):
    height, columns = matrix.shape
    width = basis.shape[1]
    blocks = columns // height
    block = pl.BlockSpec((height, height), lambda i, table: (0, table[2 * i + 1]))
    full = lambda a: pl.BlockSpec(a.shape, lambda i, table: (0, 0))
    mid = pl.BlockSpec((height, width), lambda i, table: (jnp.clip(i - 1, 0, 1), 0))
    flat_pieces = [x for pair in pieces for x in pair]
    flat_lasts = [x for pair in lasts for x in pair]
    return pl.pallas_call(
        functools.partial(update_kernel, blocks),
        grid_spec=pltpu.PrefetchScalarGridSpec(
            num_scalar_prefetch=1,
            grid=(blocks,),
            in_specs=[block, full(kept[0]), mid, full(kept[2])]
            + [full(x) for x in (total, inverse, basis, left, right)]
            + [anywhere()] * 14
            + [full(x) for x in flat_pieces[14:]]
            + [full(x) for x in flat_lasts],
            out_specs=block,
            scratch_shapes=[pltpu.VMEM((height, width), jnp.bfloat16)] * 4
            + [pltpu.VMEM((blocks, height, width // 2), jnp.float32)] * 2
            + [pltpu.SemaphoreType.DMA((blocks, 2))],
        ),
        out_shape=jax.ShapeDtypeStruct(matrix.shape, jnp.float32),
        compiler_params=PARAMS,
        cost_estimate=cost(12 * height * columns * width, 8 * height * columns),
    )(table, matrix, *kept, total, inverse, basis, left, right, *flat_pieces, *flat_lasts)


def send(pair):
    return tuple(lax.ppermute(x, AXES, ROUND) for x in pair)


def swapped(pair):
    return tuple(swap(x) for x in pair)


def half_of(pair, core):
    half = pair[0].shape[0] // 2
    return tuple(lax.dynamic_slice_in_dim(x, core * half, half, 0) for x in pair)


def ring(matrix, panel):
    core = lax.axis_index("col")
    table = jnp.asarray(order_table())[lax.axis_index("row") * 2 + core]
    middle = panel.shape[1] // 2

    def walk(own, visit):
        pieces = [own]
        here = own
        for step in range(1, 5):
            here = send(here if step < 4 else half_of(here, core))
            pieces += [here, swapped(here)]
            visit(step, pieces)
        return pieces

    state = {}

    def panel_step(step, pieces):
        flat_new = [x for pair in pieces[-2:] for x in pair]
        if step == 1:
            state["gram"] = inner(None, [*pieces[0], *flat_new])
        if step in (2, 3):
            state["gram"] = inner(state["gram"], flat_new)
        if step == 2:
            state["z"], kept = terms(table, matrix, None, pieces, 0, 1)
            state["kept"] = [kept]
        if step == 3:
            state["z"], kept = terms(table, matrix, state["z"], pieces, 1, 2)
            state["kept"].append(kept)
        if step == 4:
            state["z"], kept = terms(table, matrix, state["z"], pieces, 3, 1)
            state["kept"].append(kept)
            state["gram"] = inner(state["gram"], flat_new)

    panels = walk((panel[:, :middle], panel[:, middle:]), panel_step)
    parts = (state["z"][:, :middle], state["z"][:, middle:])
    image = tuple(x + swap(x) for x in parts)
    inverse = inverse_factor(state["gram"])
    basis, left, right = lefts(panel, image, inverse)

    def image_step(step, pieces):
        flat_new = [x for pair in pieces[-2:] for x in pair]
        if step == 1:
            other = [x for pair in panels[:3] for x in pair]
            state["inner"] = inner(None, other, [*image, *flat_new])
        elif step < 4:
            other = [x for pair in panels[2 * step - 1 : 2 * step + 1] for x in pair]
            state["inner"] = inner(state["inner"], other, flat_new)

    images = walk(image, image_step)
    updated = update(
        table, matrix, state["kept"], state["inner"], inverse, basis, left, right,
        images, panels[7:],
    )
    return (updated, basis)


def solution(mesh):
    count, cores = mesh.shape["row"], mesh.shape["col"]
    return jax.shard_map(
        ring if (count, cores) == (len(WALK), 2) else plain,
        mesh=mesh,
        in_specs=(P(("grp", "row"), "col"), P(("grp", "row"), None)),
        out_specs=(P(("grp", "row"), "col"), P(("grp", "row"), None)),
        check_vma=False,
    )
```

```python
import functools

import jax
import jax.numpy as jnp
import numpy as np
from jax import lax
from jax.experimental import pallas as pl
from jax.experimental.pallas import tpu as pltpu
from jax.sharding import PartitionSpec as P

WALK = (0, 2, 4, 6, 7, 5, 3, 1)
FULL = lax.Precision.HIGHEST
THREE = lax.Precision.HIGH


def dot(a, b, dims=((1,), (0,)), precision=FULL):
    return lax.dot_general(
        a, b, (dims, ((), ())), precision=precision, preferred_element_type=jnp.float32
    )


def swap(x):
    return lax.ppermute(x, "col", ((0, 1), (1, 0)))


def gather(part):
    return lax.all_gather(part, "row", axis=0)


def columns(halves, core):
    count, height, width = halves.shape
    mine = lax.dynamic_slice_in_dim(halves, core * (count // 2), count // 2, 0)
    other = lax.dynamic_slice_in_dim(halves, (1 - core) * (count // 2), count // 2, 0)
    other = swap(other)
    first = jnp.where(core == 0, mine, other)
    second = jnp.where(core == 0, other, mine)
    return jnp.concatenate([first[:, None], second[:, None]], 1).reshape(-1, width)


def both(core, mine, other):
    return jnp.concatenate(
        [jnp.where(core == 0, mine, other), jnp.where(core == 0, other, mine)], 0
    )


def plain(matrix, panel):
    core = lax.axis_index("col")
    height, width = panel.shape
    half = height // 2
    panel_half = lax.dynamic_slice_in_dim(panel, core * half, half, 0)
    panel_halves = gather(panel_half)
    flat = panel_halves.reshape(-1, width)
    gram = dot(flat, flat, ((0,), (0,)))
    gram = gram + swap(gram)
    panel_cols = columns(panel_halves, core)
    terms = dot(matrix, panel_cols, precision=THREE)
    mine = lax.dynamic_slice_in_dim(terms, core * half, half, 0)
    other = lax.dynamic_slice_in_dim(terms, (1 - core) * half, half, 0)
    image_half = mine + swap(other)
    image_halves = gather(image_half)

    lower = lax.linalg.cholesky(gram, symmetrize_input=False)
    inverse = lax.linalg.triangular_solve(
        lower, jnp.eye(width, dtype=jnp.float32), left_side=True, lower=True
    )
    basis = dot(panel, inverse, ((1,), (1,)))
    left = dot(2.0 * basis, inverse)
    image = both(core, image_half, swap(image_half))
    image = dot(image, inverse, ((1,), (1,)))

    flat_image = image_halves.reshape(-1, width)
    inner = dot(flat, flat_image, ((0,), (0,)))
    inner = inner + swap(inner)
    image_cols = columns(image_halves, core)
    coupling = dot(dot(inverse, inner), inverse, ((1,), (1,)))
    right = dot(2.0 * image - 4.0 * dot(basis, coupling), inverse)
    updated = matrix - dot(
        jnp.concatenate([left, right], 1),
        jnp.concatenate([image_cols, panel_cols], 1),
        ((1,), (1,)),
        THREE,
    )
    return (updated, basis)


AXES = ("row", "col")
COUNT = len(WALK)


def flat(place, core):
    return WALK[place % COUNT] * 2 + core


ROUND = tuple((flat(i, 0), flat(i + 1, 0)) for i in range(COUNT)) + tuple(
    (flat(i, 1), flat(i - 1, 1)) for i in range(COUNT)
)


def order_table():
    table = np.zeros((COUNT, 2, 4, 2), np.int32)
    for row in range(COUNT):
        place = WALK.index(row)
        for core in range(2):
            away = -1 if core == 0 else 1
            found = []
            for piece in range(COUNT):
                step, first = (piece + 1) // 2, piece % 2 == 1
                origin = WALK[(place + (away if first else -away) * step) % COUNT]
                if origin // 4 == core:
                    found.append((step, piece, origin % 4))
            found.sort()
            for k, (_, piece, block) in enumerate(found):
                table[row, core, k] = piece, block
    return table.reshape(COUNT * 2, 8)


def split(x):
    high = x.astype(jnp.bfloat16)
    return high, (x - high.astype(jnp.float32)).astype(jnp.bfloat16)


def dot3(a, b, dims=((1,), (0,))):
    one = lambda x, y: lax.dot_general(
        x, y, (dims, ((), ())), preferred_element_type=jnp.float32
    )
    return one(a[0], b[0]) + (one(a[0], b[1]) + one(a[1], b[0]))


TURNED = ((0,), (0,))
ACROSS = ((1,), (1,))


def wide(pieces):
    return jnp.concatenate([x[...] for x in pieces], 1)


def cost(flops, bytes_accessed):
    return pl.CostEstimate(
        flops=int(flops), bytes_accessed=int(bytes_accessed), transcendentals=0
    )


def vmem():
    return pl.BlockSpec(memory_space=pltpu.VMEM)


def anywhere():
    return pl.BlockSpec(memory_space=pl.ANY)


def params(mib):
    return pltpu.CompilerParams(vmem_limit_bytes=mib * 1024 * 1024)


def in_order(one, two):
    first = lax.axis_index("col") == 0
    one, two = one[...], two[...]
    return jnp.concatenate([jnp.where(first, one, two), jnp.where(first, two, one)], 1)


def inner_kernel(start, count, last, *refs):
    total, pieces, out = refs[:start], refs[start:-1], refs[-1]
    acc = total[0][...] if start else None
    lefts, rights = pieces[:count], pieces[count:]
    for i in range(0, count, 2):
        join = in_order if last and i == count - 2 else lambda *x: wide(x)
        left = join(*lefts[i : i + 2])
        right = join(*rights[i : i + 2]) if rights else left
        term = dot(left, right, TURNED)
        acc = term if acc is None else acc + term
    out[...] = acc


def inner(total, lefts, rights=(), last=False):
    lefts = [x for pair in lefts for x in pair]
    rights = [x for pair in rights for x in pair]
    width = 2 * lefts[0].shape[1]
    rows = sum(x.shape[0] for x in lefts[::2])
    args = ([] if total is None else [total]) + lefts + rights
    return pl.pallas_call(
        functools.partial(
            inner_kernel, 0 if total is None else 1, len(lefts), last
        ),
        out_shape=jax.ShapeDtypeStruct((width, width), jnp.float32),
        in_specs=[vmem()] * len(args),
        out_specs=vmem(),
        compiler_params=params(12),
        cost_estimate=cost(12 * rows * width * width, 8 * rows * width),
    )(*args)


def fetch(pieces, which, lands, sems):
    core = lax.axis_index("col")
    for index, pair in enumerate(pieces):
        turns = ((0, 1), (1, 0)) if index == COUNT - 1 else ((0, 1),)
        for turn, sides in enumerate(turns):
            here = which == index
            if len(turns) > 1:
                here = jnp.logical_and(here, core == turn)

            @pl.when(here)
            def _():
                for source, side in enumerate(sides):
                    pltpu.make_async_copy(
                        pair[source], lands[side], sems.at[side]
                    ).start()


def landed(lands, sems):
    for side in range(2):
        pltpu.make_async_copy(lands[side], lands[side], sems.at[side]).wait()


def pair_up(refs):
    return [refs[i : i + 2] for i in range(0, len(refs), 2)]


def term_kernel(first, count, *refs):
    table, matrix = refs[:2]
    refs = refs[2:]
    start = 1 if first else 0
    total, refs = refs[:start], refs[start:]
    pieces, (out, kept, land, other, sems) = pair_up(refs[:count]), refs[count:]
    step = pl.program_id(0)
    lands = (land, other)
    fetch(pieces, table[2 * (first + step)], lands, sems)
    left = split(matrix[...])

    @pl.when(step == 0)
    def _():
        out[...] = total[0][...] if start else jnp.zeros_like(out)

    landed(lands, sems)
    rows = wide(lands)
    kept[...] = rows
    out[...] += dot3(left, split(rows))


def terms(table, matrix, total, pieces, first, blocks):
    height = matrix.shape[0]
    width = 2 * pieces[0][0].shape[1]
    flat_pieces = [x for pair in pieces for x in pair]
    block = pl.BlockSpec(
        (height, height), lambda i, table: (0, table[2 * (first + i) + 1])
    )
    fixed = pl.BlockSpec((height, width), lambda i, table: (0, 0))
    begin = [] if total is None else [total]
    return pl.pallas_call(
        functools.partial(term_kernel, first, len(flat_pieces)),
        grid_spec=pltpu.PrefetchScalarGridSpec(
            num_scalar_prefetch=1,
            grid=(blocks,),
            in_specs=[block] + [fixed] * len(begin) + [anywhere()] * len(flat_pieces),
            out_specs=[fixed, pl.BlockSpec((height, width), lambda i, table: (i, 0))],
            scratch_shapes=[pltpu.VMEM((height, width // 2), jnp.float32)] * 2
            + [pltpu.SemaphoreType.DMA((2,))],
        ),
        out_shape=[
            jax.ShapeDtypeStruct((height, width), jnp.float32),
            jax.ShapeDtypeStruct((blocks * height, width), jnp.float32),
        ],
        compiler_params=params(20),
        cost_estimate=cost(
            6 * blocks * height * height * width, 4 * blocks * height * height
        ),
    )(table, matrix, *begin, *flat_pieces)


def factor(gram_ref, out, work, rows, block=64, group=8):
    size = gram_ref.shape[0]
    work[...] = gram_ref[...]
    line = lax.broadcasted_iota(jnp.int32, (size, size), 0)
    lane = lax.broadcasted_iota(jnp.int32, (size, size), 1)
    rows[...] = jnp.where(line == lane, 1.0, 0.0).astype(jnp.float32)
    index = lax.broadcasted_iota(jnp.int32, (block, 128), 0)
    for top in range(0, size, block):
        low = top // 128 * 128
        high = low + 128
        strip = jnp.concatenate(
            [work[top : top + block, low:], rows[top : top + block, :high]], 1
        )
        tiles = strip.shape[1] // 128
        spread = lambda x: jnp.concatenate([x] * tiles, 1)
        pivots = jnp.ones((block, 128), jnp.float32)
        for j in range(0, block, group):
            at = top - low + j
            some = range(group)
            down = [
                jnp.broadcast_to(strip[:, at + m : at + m + 1], (block, 128))
                for m in some
            ]
            along = [strip[j + m : j + m + 1, :] for m in some]
            cell = {
                (m, i): jnp.broadcast_to(
                    strip[j + m : j + m + 1, at + i : at + i + 1], (1, 128)
                )
                for m in some
                for i in range(m, group)
            }
            for m in some:
                over = 1.0 / cell[m, m]
                pivots = jnp.where(index == j + m, cell[m, m], pivots)
                row = along[m] * spread(over)
                strip = strip - spread(jnp.where(index > j + m, down[m], 0.0)) * row
                for i in range(m + 1, group):
                    ratio = cell[m, i] * over
                    along[i] = along[i] - spread(cell[m, i]) * row
                    down[i] = down[i] - down[m] * ratio
                    for h in range(i, group):
                        cell[i, h] = cell[i, h] - cell[m, h] * ratio
        strip = strip * spread(lax.rsqrt(pivots))
        out[top : top + block, :high] = strip[:, size - low :]
        if high < size:
            out[top : top + block, high:] = jnp.zeros(
                (block, size - high), jnp.float32
            )
        after = top + block
        if after < size:
            base = after // 128 * 128
            update = dot(strip[:, base - low : size - low], strip[:, base - low :], TURNED)
            update = update[after - base :]
            work[after:, base:] -= update[:, : size - base]
            rows[after:, :high] -= update[:, size - base :]


def factor_kernel(gram, out, work, rows):
    factor(gram, out, work, rows)


def inverse_factor(gram):
    size = gram.shape[0]
    return pl.pallas_call(
        factor_kernel,
        out_shape=jax.ShapeDtypeStruct((size, size), jnp.float32),
        in_specs=[vmem()],
        out_specs=vmem(),
        scratch_shapes=[pltpu.VMEM((size, size), jnp.float32)] * 2,
        compiler_params=params(6),
        cost_estimate=cost(10e-6 * 1e15, 4 * size * size),
    )(gram)


def left_kernel(panel, image0, image1, inverse, basis, left, right):
    inv = inverse[...]
    rows = dot(panel[...], inv, ACROSS)
    basis[...] = rows
    left[...] = dot(2.0 * rows, inv)
    right[...] = dot(2.0 * dot(wide((image0, image1)), inv, ACROSS), inv)


def lefts(panel, images, inverse):
    height, width = panel.shape
    return pl.pallas_call(
        left_kernel,
        out_shape=[jax.ShapeDtypeStruct((height, width), jnp.float32)] * 3,
        in_specs=[vmem()] * 4,
        out_specs=[vmem()] * 3,
        compiler_params=params(14),
        cost_estimate=cost(48 * height * width * width, 20 * height * width),
    )(panel, *images, inverse)


def update_kernel(blocks, *refs):
    table, matrix, kept0, kept1, kept2, total, inverse, basis, left, right = refs[:10]
    pieces, last, this = pair_up(refs[10:26]), refs[26:28], refs[28:30]
    out, one, two, three, four, land, other, sems = refs[30:]
    step = pl.program_id(0)
    width = basis.shape[1]
    slots = lambda k: (land.at[k], other.at[k])

    @pl.when(step == 0)
    def _():
        for k in range(blocks):
            fetch(pieces, table[2 * k], slots(k), sems.at[k])
        acc = total[...] + dot(in_order(*last), in_order(*this), TURNED)
        inv = inverse[...]
        coupling = dot(dot(inv, acc), inv, ACROSS)
        y = right[...] - dot(basis[...], dot(4.0 * coupling, inv))
        one[...], two[...] = split(left[...])
        three[...], four[...] = split(y)

    kept = jnp.where(step == 0, kept0[...], jnp.where(step == 3, kept2[...], kept1[...]))
    lands = (land.at[step], other.at[step])
    landed(lands, sems.at[step])
    part = dot3((three[...], four[...]), split(kept), ACROSS)
    part += dot3((one[...], two[...]), split(wide(lands)), ACROSS)
    out[...] = matrix[...] - part


def update(table, matrix, kept, total, inverse, basis, left, right, pieces, last):
    height, columns = matrix.shape
    width = basis.shape[1]
    blocks = columns // height
    block = pl.BlockSpec((height, height), lambda i, table: (0, table[2 * i + 1]))
    full = lambda a: pl.BlockSpec(a.shape, lambda i, table: (0, 0))
    mid = pl.BlockSpec((height, width), lambda i, table: (jnp.clip(i - 1, 0, 1), 0))
    flat_pieces = [x for pair in pieces for x in pair]
    return pl.pallas_call(
        functools.partial(update_kernel, blocks),
        grid_spec=pltpu.PrefetchScalarGridSpec(
            num_scalar_prefetch=1,
            grid=(blocks,),
            in_specs=[block, full(kept[0]), mid, full(kept[2])]
            + [full(x) for x in (total, inverse, basis, left, right)]
            + [anywhere()] * len(flat_pieces)
            + [full(x) for x in (*last, *pieces[-1])],
            out_specs=block,
            scratch_shapes=[pltpu.VMEM((height, width), jnp.bfloat16)] * 4
            + [pltpu.VMEM((blocks, height, width // 2), jnp.float32)] * 2
            + [pltpu.SemaphoreType.DMA((blocks, 2))],
        ),
        out_shape=jax.ShapeDtypeStruct(matrix.shape, jnp.float32),
        compiler_params=params(30),
        cost_estimate=cost(12 * height * columns * width, 8 * height * columns),
    )(table, matrix, *kept, total, inverse, basis, left, right, *flat_pieces, *last, *pieces[-1])


def send(pair):
    return tuple(lax.ppermute(x, AXES, ROUND) for x in pair)


def swapped(pair):
    return tuple(swap(x) for x in pair)


def ring(matrix, panel):
    core = lax.axis_index("col")
    table = jnp.asarray(order_table())[lax.axis_index("row") * 2 + core]
    middle = panel.shape[1] // 2

    def walk(own, visit):
        pieces = [own]
        here, ready, before = own, None, None
        for step in range(1, 5):
            if ready is not None:
                here = lax.optimization_barrier((*here, *ready))[:2]
            if step < 4:
                here = send(here)
                pieces += [here, swapped(here)]
            else:
                here = lax.ppermute(jnp.where(core == 0, *here), AXES, ROUND)
                pieces.append((here, swap(here)))
            ready, before = before, visit(step, pieces)
        return pieces

    state = {}

    def panel_step(step, pieces):
        if step == 1:
            state["gram"] = inner(None, pieces[:3])
        else:
            state["gram"] = inner(state["gram"], pieces[2 * step - 1 :], last=step == 4)
        if step > 1:
            first, blocks = ((0, 1), (1, 2), (3, 1))[step - 2]
            start = state["z"] if step > 2 else None
            state["z"], kept = terms(table, matrix, start, pieces, first, blocks)
            state.setdefault("kept", []).append(kept)
        return tuple(state[name] for name in ("gram", "z") if name in state)

    panels = walk((panel[:, :middle], panel[:, middle:]), panel_step)
    parts = (state["z"][:, :middle], state["z"][:, middle:])
    image = tuple(x + swap(x) for x in parts)
    inverse = inverse_factor(state["gram"])
    basis, left, right = lefts(panel, image, inverse)

    def image_step(step, pieces):
        if step == 1:
            state["inner"] = inner(None, panels[:3], pieces)
            return (inverse,)
        if step < 4:
            span = slice(2 * step - 1, 2 * step + 1)
            state["inner"] = inner(state["inner"], panels[span], pieces[span])
        return (state["inner"],)

    images = walk(image, image_step)
    updated = update(
        table, matrix, state["kept"], state["inner"], inverse, basis, left, right,
        images, panels[7],
    )
    return (updated, basis)


def solution(mesh):
    count, cores = mesh.shape["row"], mesh.shape["col"]
    return jax.shard_map(
        ring if (count, cores) == (len(WALK), 2) else plain,
        mesh=mesh,
        in_specs=(P(("grp", "row"), "col"), P(("grp", "row"), None)),
        out_specs=(P(("grp", "row"), "col"), P(("grp", "row"), None)),
        check_vma=False,
    )
```

```python
import functools

import jax
import jax.numpy as jnp
import numpy as np
from jax import lax
from jax.experimental import pallas as pl
from jax.experimental.pallas import tpu as pltpu
from jax.sharding import PartitionSpec as P

WALK = (0, 2, 4, 6, 7, 5, 3, 1)
FULL = lax.Precision.HIGHEST
THREE = lax.Precision.HIGH


def dot(a, b, dims=((1,), (0,)), precision=FULL):
    return lax.dot_general(
        a, b, (dims, ((), ())), precision=precision, preferred_element_type=jnp.float32
    )


def swap(x):
    return lax.ppermute(x, "col", ((0, 1), (1, 0)))


def gather(part):
    return lax.all_gather(part, "row", axis=0)


def columns(halves, core):
    count, height, width = halves.shape
    mine = lax.dynamic_slice_in_dim(halves, core * (count // 2), count // 2, 0)
    other = lax.dynamic_slice_in_dim(halves, (1 - core) * (count // 2), count // 2, 0)
    other = swap(other)
    first = jnp.where(core == 0, mine, other)
    second = jnp.where(core == 0, other, mine)
    return jnp.concatenate([first[:, None], second[:, None]], 1).reshape(-1, width)


def both(core, mine, other):
    return jnp.concatenate(
        [jnp.where(core == 0, mine, other), jnp.where(core == 0, other, mine)], 0
    )


def plain(matrix, panel):
    core = lax.axis_index("col")
    height, width = panel.shape
    half = height // 2
    panel_half = lax.dynamic_slice_in_dim(panel, core * half, half, 0)
    panel_halves = gather(panel_half)
    flat = panel_halves.reshape(-1, width)
    gram = dot(flat, flat, ((0,), (0,)))
    gram = gram + swap(gram)
    panel_cols = columns(panel_halves, core)
    terms = dot(matrix, panel_cols, precision=THREE)
    mine = lax.dynamic_slice_in_dim(terms, core * half, half, 0)
    other = lax.dynamic_slice_in_dim(terms, (1 - core) * half, half, 0)
    image_half = mine + swap(other)
    image_halves = gather(image_half)

    lower = lax.linalg.cholesky(gram, symmetrize_input=False)
    inverse = lax.linalg.triangular_solve(
        lower, jnp.eye(width, dtype=jnp.float32), left_side=True, lower=True
    )
    basis = dot(panel, inverse, ((1,), (1,)))
    left = dot(2.0 * basis, inverse)
    image = both(core, image_half, swap(image_half))
    image = dot(image, inverse, ((1,), (1,)))

    flat_image = image_halves.reshape(-1, width)
    inner = dot(flat, flat_image, ((0,), (0,)))
    inner = inner + swap(inner)
    image_cols = columns(image_halves, core)
    coupling = dot(dot(inverse, inner), inverse, ((1,), (1,)))
    right = dot(2.0 * image - 4.0 * dot(basis, coupling), inverse)
    updated = matrix - dot(
        jnp.concatenate([left, right], 1),
        jnp.concatenate([image_cols, panel_cols], 1),
        ((1,), (1,)),
        THREE,
    )
    return (updated, basis)


AXES = ("row", "col")
COUNT = len(WALK)


def flat(place, core):
    return WALK[place % COUNT] * 2 + core


ROUND = tuple((flat(i, 0), flat(i + 1, 0)) for i in range(COUNT)) + tuple(
    (flat(i, 1), flat(i - 1, 1)) for i in range(COUNT)
)


def order_table():
    table = np.zeros((COUNT, 2, 4, 2), np.int32)
    for row in range(COUNT):
        place = WALK.index(row)
        for core in range(2):
            away = -1 if core == 0 else 1
            found = []
            for piece in range(COUNT):
                step, first = (piece + 1) // 2, piece % 2 == 1
                origin = WALK[(place + (away if first else -away) * step) % COUNT]
                if origin // 4 == core:
                    found.append((step, piece, origin % 4))
            found.sort()
            for k, (_, piece, block) in enumerate(found):
                table[row, core, k] = piece, block
    return table.reshape(COUNT * 2, 8)


def split(x):
    high = x.astype(jnp.bfloat16)
    return high, (x - high.astype(jnp.float32)).astype(jnp.bfloat16)


def dot3(a, b, dims=((1,), (0,))):
    one = lambda x, y: lax.dot_general(
        x, y, (dims, ((), ())), preferred_element_type=jnp.float32
    )
    return one(a[0], b[0]) + (one(a[0], b[1]) + one(a[1], b[0]))


TURNED = ((0,), (0,))
ACROSS = ((1,), (1,))


def wide(pieces):
    return jnp.concatenate([x[...] for x in pieces], 1)


def cost(flops, bytes_accessed):
    return pl.CostEstimate(
        flops=int(flops), bytes_accessed=int(bytes_accessed), transcendentals=0
    )


def vmem():
    return pl.BlockSpec(memory_space=pltpu.VMEM)


def anywhere():
    return pl.BlockSpec(memory_space=pl.ANY)


def params(mib):
    return pltpu.CompilerParams(vmem_limit_bytes=mib * 1024 * 1024)


def in_order(one, two):
    first = lax.axis_index("col") == 0
    one, two = one[...], two[...]
    return jnp.concatenate([jnp.where(first, one, two), jnp.where(first, two, one)], 1)


def inner_kernel(start, count, last, *refs):
    total, pieces, out = refs[:start], refs[start:-1], refs[-1]
    acc = total[0][...] if start else None
    lefts, rights = pieces[:count], pieces[count:]
    for i in range(0, count, 2):
        join = in_order if last and i == count - 2 else lambda *x: wide(x)
        left = join(*lefts[i : i + 2])
        right = join(*rights[i : i + 2]) if rights else left
        if rights:
            term = dot3(split(left), split(right), TURNED)
        else:
            term = dot(left, right, TURNED)
        acc = term if acc is None else acc + term
    out[...] = acc


def inner(total, lefts, rights=(), last=False):
    lefts = [x for pair in lefts for x in pair]
    rights = [x for pair in rights for x in pair]
    width = 2 * lefts[0].shape[1]
    rows = sum(x.shape[0] for x in lefts[::2])
    args = ([] if total is None else [total]) + lefts + rights
    return pl.pallas_call(
        functools.partial(
            inner_kernel, 0 if total is None else 1, len(lefts), last
        ),
        out_shape=jax.ShapeDtypeStruct((width, width), jnp.float32),
        in_specs=[vmem()] * len(args),
        out_specs=vmem(),
        compiler_params=params(12),
        cost_estimate=cost(12 * rows * width * width, 8 * rows * width),
    )(*args)


def fetch(pieces, which, lands, sems):
    core = lax.axis_index("col")
    for index, pair in enumerate(pieces):
        turns = ((0, 1), (1, 0)) if index == COUNT - 1 else ((0, 1),)
        for turn, sides in enumerate(turns):
            here = which == index
            if len(turns) > 1:
                here = jnp.logical_and(here, core == turn)

            @pl.when(here)
            def _():
                for source, side in enumerate(sides):
                    pltpu.make_async_copy(
                        pair[source], lands[side], sems.at[side]
                    ).start()


def landed(lands, sems):
    for side in range(2):
        pltpu.make_async_copy(lands[side], lands[side], sems.at[side]).wait()


def pair_up(refs):
    return [refs[i : i + 2] for i in range(0, len(refs), 2)]


def load_kernel(matrix, high, low):
    high[...], low[...] = split(matrix[...])


def load(matrix):
    height, columns = matrix.shape
    block = pl.BlockSpec((height, height), lambda i: (0, i))
    return pl.pallas_call(
        load_kernel,
        grid=(columns // height,),
        in_specs=[block],
        out_specs=[block] * 2,
        out_shape=[jax.ShapeDtypeStruct(matrix.shape, jnp.bfloat16)] * 2,
        compiler_params=params(18),
        cost_estimate=cost(height * columns, 8 * height * columns),
    )(matrix)


def term_kernel(first, blocks, count, *refs):
    table, high, low = refs[:3]
    refs = refs[3:]
    start = 2 if first else 0
    total, refs = refs[:start], refs[start:]
    pieces, (out0, out1, kept_high, kept_low, land, other, sems) = (
        pair_up(refs[:count]),
        refs[count:],
    )
    height, middle = out0.shape
    slots = [((land.at[k], other.at[k]), sems.at[k]) for k in range(blocks)]
    for k in range(blocks):
        fetch(pieces, table[2 * (first + k)], *slots[k])
    acc = wide(total) if start else None
    for k in range(blocks):
        landed(*slots[k])
        right = split(wide(slots[k][0]))
        rows = slice(k * height, k * height + height)
        kept_high[rows], kept_low[rows] = right
        at = pl.multiple_of(table[2 * (first + k) + 1] * height, height)
        term = dot3((high[:, pl.ds(at, height)], low[:, pl.ds(at, height)]), right)
        acc = term if acc is None else acc + term
    out0[...], out1[...] = acc[:, :middle], acc[:, middle:]


def terms(table, halves, total, pieces, first, blocks):
    height = halves[0].shape[0]
    middle = pieces[0][0].shape[1]
    width = 2 * middle
    flat_pieces = [x for pair in pieces for x in pair]
    begin = [] if total is None else list(total)
    *total, high, low = pl.pallas_call(
        functools.partial(term_kernel, first, blocks, len(flat_pieces)),
        in_specs=[pl.BlockSpec(memory_space=pltpu.SMEM)]
        + [vmem()] * (2 + len(begin))
        + [anywhere()] * len(flat_pieces),
        out_specs=[vmem()] * 4,
        scratch_shapes=[pltpu.VMEM((blocks, height, middle), jnp.float32)] * 2
        + [pltpu.SemaphoreType.DMA((blocks, 2))],
        out_shape=[jax.ShapeDtypeStruct((height, middle), jnp.float32)] * 2
        + [jax.ShapeDtypeStruct((blocks * height, width), jnp.bfloat16)] * 2,
        compiler_params=params(16),
        cost_estimate=cost(
            6 * blocks * height * height * width, 4 * blocks * height * height
        ),
    )(table, *halves, *begin, *flat_pieces)
    return total, (high, low)


def factor(out, work, rows, tops, block=64, group=8):
    size = out.shape[0]
    index = lax.broadcasted_iota(jnp.int32, (block, 128), 0)
    for top in tops:
        low = top // 128 * 128
        high = low + 128
        strip = jnp.concatenate(
            [work[top : top + block, low:], rows[top : top + block, :high]], 1
        )
        tiles = strip.shape[1] // 128
        spread = lambda x: jnp.concatenate([x] * tiles, 1)
        pivots = jnp.ones((block, 128), jnp.float32)
        for j in range(0, block, group):
            at = top - low + j
            some = range(group)
            down = [
                jnp.broadcast_to(strip[:, at + m : at + m + 1], (block, 128))
                for m in some
            ]
            along = [strip[j + m : j + m + 1, :] for m in some]
            cell = {
                (m, i): jnp.broadcast_to(
                    strip[j + m : j + m + 1, at + i : at + i + 1], (1, 128)
                )
                for m in some
                for i in range(m, group)
            }
            for m in some:
                over = 1.0 / cell[m, m]
                pivots = jnp.where(index == j + m, cell[m, m], pivots)
                row = along[m] * spread(over)
                strip = strip - spread(jnp.where(index > j + m, down[m], 0.0)) * row
                for i in range(m + 1, group):
                    ratio = cell[m, i] * over
                    along[i] = along[i] - spread(cell[m, i]) * row
                    down[i] = down[i] - down[m] * ratio
                    for h in range(i, group):
                        cell[i, h] = cell[i, h] - cell[m, h] * ratio
        strip = strip * spread(lax.rsqrt(pivots))
        out[top : top + block, :high] = strip[:, size - low :]
        if high < size:
            out[top : top + block, high:] = jnp.zeros(
                (block, size - high), jnp.float32
            )
        after = top + block
        if after < size:
            base = after // 128 * 128
            update = dot(strip[:, base - low : size - low], strip[:, base - low :], TURNED)
            update = update[after - base :]
            work[after:, base:] -= update[:, : size - base]
            rows[after:, :high] -= update[:, size - base :]


def first_kernel(gram, out, work, rows):
    size = gram.shape[0]
    work[...] = gram[...]
    line = lax.broadcasted_iota(jnp.int32, (size, size), 0)
    lane = lax.broadcasted_iota(jnp.int32, (size, size), 1)
    rows[...] = jnp.where(line == lane, 1.0, 0.0).astype(jnp.float32)
    factor(out, work, rows, range(0, size // 2, 64))
    out[size // 2 :, :] = jnp.zeros((size // 2, size), jnp.float32)


def second_kernel(begun, work_in, rows_in, out, work, rows):
    size = out.shape[0]
    work[...] = work_in[...]
    rows[...] = rows_in[...]
    out[...] = begun[...]
    factor(out, work, rows, range(size // 2, size, 64))


def factor_call(kernel, args, scratch):
    size = args[0].shape[0]
    shape = (size, size)
    outs = 1 if scratch else 3
    return pl.pallas_call(
        kernel,
        out_shape=[jax.ShapeDtypeStruct(shape, jnp.float32)] * outs,
        in_specs=[vmem()] * len(args),
        out_specs=[vmem()] * outs,
        scratch_shapes=[pltpu.VMEM(shape, jnp.float32)] * scratch,
        compiler_params=params(6),
        cost_estimate=cost(4e9, 4 * size * size),
    )(*args)


def left_kernel(panel, image0, image1, inverse, basis, left, right):
    inv = inverse[...]
    rows = dot(panel[...], inv, ACROSS)
    basis[...] = rows
    inv = split(inv)
    left[...] = dot3(split(2.0 * rows), inv)
    image = dot3(split(wide((image0, image1))), inv, ACROSS)
    right[...] = dot3(split(2.0 * image), inv)


def lefts(panel, images, inverse):
    height, width = panel.shape
    return pl.pallas_call(
        left_kernel,
        out_shape=[jax.ShapeDtypeStruct((height, width), jnp.float32)] * 3,
        in_specs=[vmem()] * 4,
        out_specs=[vmem()] * 3,
        compiler_params=params(14),
        cost_estimate=cost(48 * height * width * width, 20 * height * width),
    )(panel, *images, inverse)


def before_kernel(count, *refs):
    table, matrix, left = refs[:3]
    pieces, (out, land, other, sems) = pair_up(refs[3 : 3 + count]), refs[3 + count :]
    lands = (land, other)
    fetch(pieces, table[2 * pl.program_id(0)], lands, sems)
    one = split(left[...])
    landed(lands, sems)
    out[...] = matrix[...] - dot3(one, split(wide(lands)), ACROSS)


def before(table, matrix, left, pieces, blocks):
    height, width = left.shape
    flat_pieces = [x for pair in pieces for x in pair]
    block = pl.BlockSpec((height, height), lambda i, table: (0, table[2 * i + 1]))
    return pl.pallas_call(
        functools.partial(before_kernel, len(flat_pieces)),
        grid_spec=pltpu.PrefetchScalarGridSpec(
            num_scalar_prefetch=1,
            grid=(blocks,),
            in_specs=[block, pl.BlockSpec(left.shape, lambda i, table: (0, 0))]
            + [anywhere()] * len(flat_pieces),
            out_specs=pl.BlockSpec((height, height), lambda i, table: (0, i)),
            scratch_shapes=[pltpu.VMEM((height, width // 2), jnp.float32)] * 2
            + [pltpu.SemaphoreType.DMA((2,))],
        ),
        out_shape=jax.ShapeDtypeStruct((height, blocks * height), jnp.float32),
        compiler_params=params(20),
        cost_estimate=cost(
            6 * blocks * height * height * width, 8 * blocks * height * height
        ),
    )(table, matrix, left, *flat_pieces)


def update_kernel(last, *refs):
    table, matrix, early, total, inverse, basis, left, right = refs[:8]
    kept, pieces = refs[8:14], pair_up(refs[14:30])
    panel_last, image_last = refs[30:32], refs[32:34]
    out, three, four, land, other, sems = refs[34:]
    step = pl.program_id(0)
    lands = (land, other)

    @pl.when(step == 0)
    def _():
        fetch(pieces, table[2 * last], lands, sems)
        acc = total[...] + dot3(
            split(in_order(*panel_last)), split(in_order(*image_last)), TURNED
        )
        inv = inverse[...]
        coupling = dot(dot(inv, acc), inv, ACROSS)
        y = right[...] - dot(basis[...], dot(4.0 * coupling, inv))
        three[...], four[...] = split(y)
        landed(lands, sems)

    def less(high, low):
        return dot3((three[...], four[...]), (high[...], low[...]), ACROSS)

    @pl.when(step == 0)
    def _():
        part = less(kept[4], kept[5])
        part += dot3(split(left[...]), split(wide(lands)), ACROSS)
        out[...] = matrix[...] - part

    @pl.when(step == 1)
    def _():
        out[...] = early[...] - less(kept[0], kept[1])

    @pl.when(step > 1)
    def _():
        out[...] = early[...] - less(kept[2], kept[3])


def update(table, matrix, early, total, inverse, basis, left, right, kept, pieces, opposite):
    height, columns = matrix.shape
    width = basis.shape[1]
    blocks = columns // height
    last = blocks - 1
    order = lambda i: jnp.where(i == 0, last, i - 1)
    block = pl.BlockSpec(
        (height, height), lambda i, table: (0, table[2 * order(i) + 1])
    )
    full = lambda a: pl.BlockSpec(a.shape, lambda i, table: (0, 0))
    mid = pl.BlockSpec((height, width), lambda i, table: (jnp.clip(i - 2, 0, 1), 0))
    final = pl.BlockSpec((height, height), lambda i, table: (0, table[2 * last + 1]))
    done = pl.BlockSpec((height, height), lambda i, table: (0, jnp.maximum(i - 1, 0)))
    flat_pieces = [x for pair in pieces for x in pair]
    return pl.pallas_call(
        functools.partial(update_kernel, last),
        grid_spec=pltpu.PrefetchScalarGridSpec(
            num_scalar_prefetch=1,
            grid=(blocks,),
            in_specs=[final, done]
            + [full(x) for x in (total, inverse, basis, left, right)]
            + [full(kept[0][0])] * 2 + [mid] * 2 + [full(kept[2][0])] * 2
            + [anywhere()] * len(flat_pieces)
            + [full(x) for x in (*opposite, *pieces[-1])],
            out_specs=block,
            scratch_shapes=[pltpu.VMEM((height, width), jnp.bfloat16)] * 2
            + [pltpu.VMEM((height, width // 2), jnp.float32)] * 2
            + [pltpu.SemaphoreType.DMA((2,))],
        ),
        out_shape=jax.ShapeDtypeStruct(matrix.shape, jnp.float32),
        compiler_params=params(30),
        cost_estimate=cost(12 * height * columns * width, 8 * height * columns),
    )(
        table, matrix, early, total, inverse, basis, left, right,
        *(x for pair in kept for x in pair),
        *flat_pieces, *opposite, *pieces[-1],
    )


def hop(x):
    return lax.ppermute(x, AXES, ROUND)


def swapped(pair):
    return tuple(swap(x) for x in pair)


def after(x, *others):
    return lax.optimization_barrier((x, *others))[0]


def ring(matrix, panel):
    core = lax.axis_index("col")
    table = jnp.asarray(order_table())[lax.axis_index("row") * 2 + core]
    middle = panel.shape[1] // 2

    own = (panel[:, :middle], panel[:, middle:])
    halves = load(matrix)
    a1 = (hop(own[0]), hop(own[1]))
    b1 = swapped(a1)
    gram = inner(None, [own, a1, b1])
    a2 = (hop(after(a1[0], *halves)), hop(a1[1]))
    b2 = swapped(a2)
    a3 = (hop(after(a2[0], gram)), hop(a2[1]))
    b3 = swapped(a3)
    gram = inner(gram, [a2, b2])
    image, kept = terms(table, halves, None, [own, a1, b1, a2, b2], 0, 1)
    kepts = [kept]
    one = hop(jnp.where(core == 0, a3[0], after(a3[1], gram, image[0])))
    panels = [own, a1, b1, a2, b2, a3, b3]
    image, kept = terms(table, halves, image, panels, 1, 2)
    kepts.append(kept)
    opposite = (one, swap(after(one, image[0])))
    image, kept = terms(table, halves, image, [*panels, opposite], 3, 1)
    kepts.append(kept)

    image = tuple(x + swap(x) for x in image)
    gram = inner(gram, [a3, b3, opposite], last=True)
    c1 = (hop(after(image[0], gram)), hop(image[1]))
    d1 = swapped(c1)
    begun = factor_call(first_kernel, [gram], 0)
    c2 = (hop(after(c1[0], begun[0])), hop(c1[1]))
    d2 = swapped(c2)
    (inverse,) = factor_call(second_kernel, begun, 2)
    basis, left, right = lefts(panel, image, inverse)
    c3 = (hop(after(c2[0], left)), hop(c2[1]))
    d3 = swapped(c3)
    one = hop(jnp.where(core == 0, c3[0], c3[1]))
    images = [image, c1, d1, c2, d2, c3, d3]
    total = inner(None, panels, images)
    early = before(table, matrix, left, images, 3)
    last = (one, swap(after(one, total)))
    updated = update(
        table, matrix, early, total, inverse, basis, left, right, kepts,
        [*images, last], opposite,
    )
    return (updated, basis)


def solution(mesh):
    count, cores = mesh.shape["row"], mesh.shape["col"]
    return jax.shard_map(
        ring if (count, cores) == (len(WALK), 2) else plain,
        mesh=mesh,
        in_specs=(P(("grp", "row"), "col"), P(("grp", "row"), None)),
        out_specs=(P(("grp", "row"), "col"), P(("grp", "row"), None)),
        check_vma=False,
    )
```

```python
import functools

import jax
import jax.numpy as jnp
import numpy as np
from jax import lax
from jax.experimental import pallas as pl
from jax.experimental.pallas import tpu as pltpu
from jax.sharding import PartitionSpec as P

WALK = (0, 2, 4, 6, 7, 5, 3, 1)
FULL = lax.Precision.HIGHEST
THREE = lax.Precision.HIGH


def dot(a, b, dims=((1,), (0,)), precision=FULL):
    return lax.dot_general(
        a, b, (dims, ((), ())), precision=precision, preferred_element_type=jnp.float32
    )


def swap(x):
    return lax.ppermute(x, "col", ((0, 1), (1, 0)))


def gather(part):
    return lax.all_gather(part, "row", axis=0)


def columns(halves, core):
    count, height, width = halves.shape
    mine = lax.dynamic_slice_in_dim(halves, core * (count // 2), count // 2, 0)
    other = lax.dynamic_slice_in_dim(halves, (1 - core) * (count // 2), count // 2, 0)
    other = swap(other)
    first = jnp.where(core == 0, mine, other)
    second = jnp.where(core == 0, other, mine)
    return jnp.concatenate([first[:, None], second[:, None]], 1).reshape(-1, width)


def both(core, mine, other):
    return jnp.concatenate(
        [jnp.where(core == 0, mine, other), jnp.where(core == 0, other, mine)], 0
    )


def plain(matrix, panel):
    core = lax.axis_index("col")
    height, width = panel.shape
    half = height // 2
    panel_half = lax.dynamic_slice_in_dim(panel, core * half, half, 0)
    panel_halves = gather(panel_half)
    flat = panel_halves.reshape(-1, width)
    gram = dot(flat, flat, ((0,), (0,)))
    gram = gram + swap(gram)
    panel_cols = columns(panel_halves, core)
    terms = dot(matrix, panel_cols, precision=THREE)
    mine = lax.dynamic_slice_in_dim(terms, core * half, half, 0)
    other = lax.dynamic_slice_in_dim(terms, (1 - core) * half, half, 0)
    image_half = mine + swap(other)
    image_halves = gather(image_half)

    lower = lax.linalg.cholesky(gram, symmetrize_input=False)
    inverse = lax.linalg.triangular_solve(
        lower, jnp.eye(width, dtype=jnp.float32), left_side=True, lower=True
    )
    basis = dot(panel, inverse, ((1,), (1,)))
    left = dot(2.0 * basis, inverse)
    image = both(core, image_half, swap(image_half))
    image = dot(image, inverse, ((1,), (1,)))

    flat_image = image_halves.reshape(-1, width)
    inner = dot(flat, flat_image, ((0,), (0,)))
    inner = inner + swap(inner)
    image_cols = columns(image_halves, core)
    coupling = dot(dot(inverse, inner), inverse, ((1,), (1,)))
    right = dot(2.0 * image - 4.0 * dot(basis, coupling), inverse)
    updated = matrix - dot(
        jnp.concatenate([left, right], 1),
        jnp.concatenate([image_cols, panel_cols], 1),
        ((1,), (1,)),
        THREE,
    )
    return (updated, basis)


AXES = ("row", "col")
COUNT = len(WALK)


def flat(place, core):
    return WALK[place % COUNT] * 2 + core


ROUND = tuple((flat(i, 0), flat(i + 1, 0)) for i in range(COUNT)) + tuple(
    (flat(i, 1), flat(i - 1, 1)) for i in range(COUNT)
)


def order_table():
    table = np.zeros((COUNT, 2, 4, 2), np.int32)
    for row in range(COUNT):
        place = WALK.index(row)
        for core in range(2):
            away = -1 if core == 0 else 1
            found = []
            for piece in range(COUNT):
                step, first = (piece + 1) // 2, piece % 2 == 1
                origin = WALK[(place + (away if first else -away) * step) % COUNT]
                if origin // 4 == core:
                    found.append((step, piece, origin % 4))
            found.sort()
            for k, (_, piece, block) in enumerate(found):
                table[row, core, k] = piece, block
    return table.reshape(COUNT * 2, 8)


def entry(table, k):
    device = lax.axis_index("row") * 2 + lax.axis_index("col")
    return table[device, 2 * k], table[device, 2 * k + 1]


def split(x):
    high = x.astype(jnp.bfloat16)
    return high, (x - high.astype(jnp.float32)).astype(jnp.bfloat16)


def dot3(a, b, dims=((1,), (0,))):
    one = lambda x, y: lax.dot_general(
        x, y, (dims, ((), ())), preferred_element_type=jnp.float32
    )
    return one(a[0], b[0]) + (one(a[0], b[1]) + one(a[1], b[0]))


TURNED = ((0,), (0,))
ACROSS = ((1,), (1,))


def wide(pieces):
    return jnp.concatenate([x[...] for x in pieces], 1)


def cost(flops, bytes_accessed):
    return pl.CostEstimate(
        flops=int(flops), bytes_accessed=int(bytes_accessed), transcendentals=0
    )


def vmem():
    return pl.BlockSpec(memory_space=pltpu.VMEM)


def anywhere():
    return pl.BlockSpec(memory_space=pl.ANY)


def in_hbm():
    return pl.BlockSpec(memory_space=pltpu.HBM)


def in_smem():
    return pl.BlockSpec(memory_space=pltpu.SMEM)


def block_fetch(matrix, table, k, land, sem, parts=6):
    height, width = land.shape
    at = pl.multiple_of(entry(table, k)[1] * width, width)
    step = height // parts
    for low in range(0, height, step):
        pltpu.make_async_copy(
            matrix.at[pl.ds(low, step), pl.ds(at, width)],
            land.at[pl.ds(low, step)],
            sem,
        ).start()


def block_copy(out, table, k, source, sem):
    width = source.shape[1]
    at = pl.multiple_of(entry(table, k)[1] * width, width)
    return pltpu.make_async_copy(source, out.at[:, pl.ds(at, width)], sem)


def params(mib):
    return pltpu.CompilerParams(vmem_limit_bytes=mib * 1024 * 1024)


def in_order(one, two):
    first = lax.axis_index("col") == 0
    one, two = one[...], two[...]
    return jnp.concatenate([jnp.where(first, one, two), jnp.where(first, two, one)], 1)


def inner_kernel(start, count, last, *refs):
    total, pieces, out = refs[:start], refs[start:-1], refs[-1]
    acc = total[0][...] if start else None
    lefts, rights = pieces[:count], pieces[count:]
    for i in range(0, count, 2):
        join = in_order if last and i == count - 2 else lambda *x: wide(x)
        left = join(*lefts[i : i + 2])
        right = join(*rights[i : i + 2]) if rights else left
        if rights:
            term = dot3(split(left), split(right), TURNED)
        else:
            term = dot(left, right, TURNED)
        acc = term if acc is None else acc + term
    out[...] = acc


def inner(total, lefts, rights=(), last=False):
    lefts = [x for pair in lefts for x in pair]
    rights = [x for pair in rights for x in pair]
    width = 2 * lefts[0].shape[1]
    rows = sum(x.shape[0] for x in lefts[::2])
    args = ([] if total is None else [total]) + lefts + rights
    return pl.pallas_call(
        functools.partial(
            inner_kernel, 0 if total is None else 1, len(lefts), last
        ),
        out_shape=jax.ShapeDtypeStruct((width, width), jnp.float32),
        in_specs=[vmem()] * len(args),
        out_specs=vmem(),
        compiler_params=params(12),
        cost_estimate=cost(12 * rows * width * width, 8 * rows * width),
    )(*args)


def fetch(pieces, which, lands, sems):
    core = lax.axis_index("col")
    for index, pair in enumerate(pieces):
        turns = ((0, 1), (1, 0)) if index == COUNT - 1 else ((0, 1),)
        for turn, sides in enumerate(turns):
            here = which == index
            if len(turns) > 1:
                here = jnp.logical_and(here, core == turn)

            @pl.when(here)
            def _():
                for source, side in enumerate(sides):
                    pltpu.make_async_copy(
                        pair[source], lands[side], sems.at[side]
                    ).start()


def pick(pieces, which, land):
    for index, pair in enumerate(pieces):
        join = in_order if index == COUNT - 1 else lambda *x: wide(x)

        @pl.when(which == index)
        def _():
            land[...] = join(*pair)


def landed(lands, sems):
    for side in range(2):
        pltpu.make_async_copy(lands[side], lands[side], sems.at[side]).wait()


def pair_up(refs):
    return [refs[i : i + 2] for i in range(0, len(refs), 2)]


def term_kernel(first, blocks, count, *refs):
    table, matrix = refs[:2]
    refs = refs[2:]
    start = 2 if first else 0
    total, refs = refs[:start], refs[start:]
    pieces, (out0, out1, kept_high, kept_low, held, land, other, sems, held_sems) = (
        pair_up(refs[:count]),
        refs[count:],
    )
    height, middle = out0.shape
    slots = [((land.at[k], other.at[k]), sems.at[k]) for k in range(blocks)]
    for k in range(blocks):
        block_fetch(matrix, table, first + k, held.at[k], held_sems.at[k])
        fetch(pieces, entry(table, first + k)[0], *slots[k])
    acc = wide(total) if start else None
    for k in range(blocks):
        landed(*slots[k])
        right = split(wide(slots[k][0]))
        rows = slice(k * height, k * height + height)
        kept_high[rows], kept_low[rows] = right
        pltpu.make_async_copy(held.at[k], held.at[k], held_sems.at[k]).wait()
        term = dot3(split(held[k]), right)
        acc = term if acc is None else acc + term
    out0[...], out1[...] = acc[:, :middle], acc[:, middle:]


def terms(table, matrix, total, pieces, first, blocks):
    height = matrix.shape[0]
    middle = pieces[0][0].shape[1]
    width = 2 * middle
    flat_pieces = [x for pair in pieces for x in pair]
    begin = [] if total is None else list(total)
    *total, high, low = pl.pallas_call(
        functools.partial(term_kernel, first, blocks, len(flat_pieces)),
        in_specs=[in_smem(), in_hbm()]
        + [vmem()] * len(begin)
        + [anywhere()] * len(flat_pieces),
        out_specs=[vmem()] * 4,
        scratch_shapes=[pltpu.VMEM((blocks, height, height), jnp.float32)]
        + [pltpu.VMEM((blocks, height, middle), jnp.float32)] * 2
        + [pltpu.SemaphoreType.DMA((blocks, 2)), pltpu.SemaphoreType.DMA((blocks,))],
        out_shape=[jax.ShapeDtypeStruct((height, middle), jnp.float32)] * 2
        + [jax.ShapeDtypeStruct((blocks * height, width), jnp.bfloat16)] * 2,
        compiler_params=params(44),
        cost_estimate=cost(
            6 * blocks * height * height * width, 4 * blocks * height * height
        ),
    )(table, matrix, *begin, *flat_pieces)
    return total, (high, low)


def factor(out, work, rows, tops, block=64, group=8):
    size = out.shape[0]
    index = lax.broadcasted_iota(jnp.int32, (block, 128), 0)
    for top in tops:
        low = top // 128 * 128
        high = low + 128
        strip = jnp.concatenate(
            [work[top : top + block, low:], rows[top : top + block, :high]], 1
        )
        tiles = strip.shape[1] // 128
        spread = lambda x: jnp.concatenate([x] * tiles, 1)
        pivots = jnp.ones((block, 128), jnp.float32)
        for j in range(0, block, group):
            at = top - low + j
            some = range(group)
            down = [
                jnp.broadcast_to(strip[:, at + m : at + m + 1], (block, 128))
                for m in some
            ]
            along = [strip[j + m : j + m + 1, :] for m in some]
            cell = {
                (m, i): jnp.broadcast_to(
                    strip[j + m : j + m + 1, at + i : at + i + 1], (1, 128)
                )
                for m in some
                for i in range(m, group)
            }
            for m in some:
                over = 1.0 / cell[m, m]
                pivots = jnp.where(index == j + m, cell[m, m], pivots)
                row = along[m] * spread(over)
                strip = strip - spread(jnp.where(index > j + m, down[m], 0.0)) * row
                for i in range(m + 1, group):
                    ratio = cell[m, i] * over
                    along[i] = along[i] - spread(cell[m, i]) * row
                    down[i] = down[i] - down[m] * ratio
                    for h in range(i, group):
                        cell[i, h] = cell[i, h] - cell[m, h] * ratio
        strip = strip * spread(lax.rsqrt(pivots))
        out[top : top + block, :high] = strip[:, size - low :]
        if high < size:
            out[top : top + block, high:] = jnp.zeros(
                (block, size - high), jnp.float32
            )
        after = top + block
        if after < size:
            base = after // 128 * 128
            update = dot(strip[:, base - low : size - low], strip[:, base - low :], TURNED)
            update = update[after - base :]
            work[after:, base:] -= update[:, : size - base]
            rows[after:, :high] -= update[:, size - base :]


def first_kernel(gram, out, work, rows):
    size = gram.shape[0]
    work[...] = gram[...]
    line = lax.broadcasted_iota(jnp.int32, (size, size), 0)
    lane = lax.broadcasted_iota(jnp.int32, (size, size), 1)
    rows[...] = jnp.where(line == lane, 1.0, 0.0).astype(jnp.float32)
    factor(out, work, rows, range(0, size // 2, 64))
    out[size // 2 :, :] = jnp.zeros((size // 2, size), jnp.float32)


def second_kernel(begun, work_in, rows_in, out, work, rows):
    size = out.shape[0]
    work[...] = work_in[...]
    rows[...] = rows_in[...]
    out[...] = begun[...]
    factor(out, work, rows, range(size // 2, size, 64))


def factor_call(kernel, args, scratch):
    size = args[0].shape[0]
    shape = (size, size)
    outs = 1 if scratch else 3
    return pl.pallas_call(
        kernel,
        out_shape=[jax.ShapeDtypeStruct(shape, jnp.float32)] * outs,
        in_specs=[vmem()] * len(args),
        out_specs=[vmem()] * outs,
        scratch_shapes=[pltpu.VMEM(shape, jnp.float32)] * scratch,
        compiler_params=params(6),
        cost_estimate=cost(4e9, 4 * size * size),
    )(*args)


def left_kernel(panel, image0, image1, inverse, basis, left, right):
    inv = inverse[...]
    rows = dot(panel[...], inv, ACROSS)
    basis[...] = rows
    inv = split(inv)
    left[...] = dot3(split(2.0 * rows), inv)
    image = dot3(split(wide((image0, image1))), inv, ACROSS)
    right[...] = dot3(split(2.0 * image), inv)


def lefts(panel, images, inverse):
    height, width = panel.shape
    return pl.pallas_call(
        left_kernel,
        out_shape=[jax.ShapeDtypeStruct((height, width), jnp.float32)] * 3,
        in_specs=[vmem()] * 4,
        out_specs=[vmem()] * 3,
        compiler_params=params(14),
        cost_estimate=cost(48 * height * width * width, 20 * height * width),
    )(panel, *images, inverse)


def columns_of(matrix, table, k):
    width = matrix.shape[0]
    at = pl.multiple_of(entry(table, k)[1] * width, width)
    return matrix[:, pl.ds(at, width)]


def before_kernel(blocks, count, *refs):
    table, matrix, left = refs[:3]
    pieces, (out, land) = pair_up(refs[3 : 3 + count]), refs[3 + count :]
    one = split(left[...])
    for k in range(blocks):
        pick(pieces, entry(table, k)[0], land)
        right = split(land[...])
        out[k] = columns_of(matrix, table, k) - dot3(one, right, ACROSS)


def before(table, matrix, left, pieces, blocks):
    height, width = left.shape
    flat_pieces = [x for pair in pieces for x in pair]
    return pl.pallas_call(
        functools.partial(before_kernel, blocks, len(flat_pieces)),
        in_specs=[in_smem()] + [vmem()] * (2 + len(flat_pieces)),
        out_specs=vmem(),
        scratch_shapes=[pltpu.VMEM((height, width), jnp.float32)],
        out_shape=jax.ShapeDtypeStruct((blocks, height, height), jnp.float32),
        compiler_params=params(20),
        cost_estimate=cost(
            6 * blocks * height * height * width, 8 * blocks * height * height
        ),
    )(table, matrix, left, *flat_pieces)


def update_kernel(last, *refs):
    table, matrix, early, total, inverse, basis, left, right = refs[:8]
    kept, pieces = pair_up(refs[8:14]), pair_up(refs[14:30])
    panel_last, image_last = refs[30:32], pieces[-1]
    out, held, land, out_sems = refs[32:]
    height = left.shape[0]
    pick(pieces, entry(table, last)[0], land)
    acc = total[...] + dot3(
        split(in_order(*panel_last)), split(in_order(*image_last)), TURNED
    )
    inv = inverse[...]
    coupling = dot(dot(inv, acc), inv, ACROSS)
    y = right[...] - dot3(split(basis[...]), split(dot(4.0 * coupling, inv)))
    y = split(y)
    held[1] = columns_of(matrix, table, last) - dot3(
        split(left[...]), split(land[...]), ACROSS
    )
    writes = []
    for k in range(last + 1):
        high, low = kept[min(k, 1) if k < last else 2]
        rows = slice(0, height) if k in (0, last) else slice((k - 1) * height, k * height)
        if k >= 2:
            writes[k - 2].wait()
        term = dot3(y, (high[rows], low[rows]), ACROSS)
        if k < last:
            now = 0 if k % 2 == 0 else 2
        else:
            now = 1
        held[now] = (early[k] if k < last else held[1]) - term
        writes.append(
            block_copy(out, table, k, held.at[now], out_sems.at[k])
        )
        writes[-1].start()
    for write in writes[-2:]:
        write.wait()


def update(table, matrix, early, total, inverse, basis, left, right, kept, pieces, opposite):
    height, columns = matrix.shape
    width = basis.shape[1]
    blocks = columns // height
    flat_pieces = [x for pair in pieces for x in pair]
    return pl.pallas_call(
        functools.partial(update_kernel, blocks - 1),
        in_specs=[in_smem()]
        + [vmem()] * (15 + len(flat_pieces)),
        out_specs=in_hbm(),
        scratch_shapes=[
            pltpu.VMEM((3, height, height), jnp.float32),
            pltpu.VMEM((height, width), jnp.float32),
            pltpu.SemaphoreType.DMA((blocks,)),
        ],
        out_shape=jax.ShapeDtypeStruct(matrix.shape, jnp.float32),
        compiler_params=params(24),
        cost_estimate=cost(12 * height * columns * width, 8 * height * columns),
    )(
        table, matrix, early, total, inverse, basis, left, right,
        *(x for pair in kept for x in pair),
        *flat_pieces, *opposite,
    )


def hop(x):
    return lax.ppermute(x, AXES, ROUND)


def swapped(pair):
    return tuple(swap(x) for x in pair)


def after(x, *others):
    return lax.optimization_barrier((x, *others))[0]


def ring(matrix, panel):
    core = lax.axis_index("col")
    table = jnp.asarray(order_table())
    middle = panel.shape[1] // 2

    own = (panel[:, :middle], panel[:, middle:])
    a1 = (hop(own[0]), hop(own[1]))
    b1 = swapped(a1)
    gram = inner(None, [own, a1, b1])
    a2 = (hop(a1[0]), hop(a1[1]))
    b2 = swapped(a2)
    a3 = (hop(after(a2[0], gram)), hop(a2[1]))
    b3 = swapped(a3)
    gram = inner(gram, [a2, b2])
    image, kept = terms(table, matrix, None, [own, a1, b1, a2, b2], 0, 1)
    kepts = [kept]
    one = hop(jnp.where(core == 0, a3[0], after(a3[1], gram, image[0])))
    panels = [own, a1, b1, a2, b2, a3, b3]
    image, kept = terms(table, matrix, image, panels, 1, 2)
    kepts.append(kept)
    opposite = (one, swap(after(one, image[0])))
    image, kept = terms(table, matrix, image, [*panels, opposite], 3, 1)
    kepts.append(kept)

    image = tuple(x + swap(x) for x in image)
    gram = inner(gram, [a3, b3, opposite], last=True)
    c1 = (hop(after(image[0], gram)), hop(image[1]))
    d1 = swapped(c1)
    begun = factor_call(first_kernel, [gram], 0)
    c2 = (hop(after(c1[0], begun[0])), hop(c1[1]))
    d2 = swapped(c2)
    (inverse,) = factor_call(second_kernel, begun, 2)
    basis, left, right = lefts(panel, image, inverse)
    c3 = (hop(after(c2[0], left)), hop(c2[1]))
    d3 = swapped(c3)
    one = hop(jnp.where(core == 0, c3[0], c3[1]))
    images = [image, c1, d1, c2, d2, c3, d3]
    total = inner(None, panels, images)
    early = before(table, matrix, left, images, 3)
    last = (one, swap(after(one, total)))
    updated = update(
        table, matrix, early, total, inverse, basis, left, right, kepts,
        [*images, last], opposite,
    )
    return (updated, basis)


def solution(mesh):
    count, cores = mesh.shape["row"], mesh.shape["col"]
    return jax.shard_map(
        ring if (count, cores) == (len(WALK), 2) else plain,
        mesh=mesh,
        in_specs=(P(("grp", "row"), "col"), P(("grp", "row"), None)),
        out_specs=(P(("grp", "row"), "col"), P(("grp", "row"), None)),
        check_vma=False,
    )
```

```python
import functools

import jax
import jax.numpy as jnp
import numpy as np
from jax import lax
from jax.experimental import pallas as pl
from jax.experimental.pallas import tpu as pltpu
from jax.sharding import PartitionSpec as P

WALK = (0, 2, 4, 6, 7, 5, 3, 1)
FULL = lax.Precision.HIGHEST
THREE = lax.Precision.HIGH


def dot(a, b, dims=((1,), (0,)), precision=FULL):
    return lax.dot_general(
        a, b, (dims, ((), ())), precision=precision, preferred_element_type=jnp.float32
    )


def swap(x):
    return lax.ppermute(x, "col", ((0, 1), (1, 0)))


def gather(part):
    return lax.all_gather(part, "row", axis=0)


def columns(halves, core):
    count, height, width = halves.shape
    mine = lax.dynamic_slice_in_dim(halves, core * (count // 2), count // 2, 0)
    other = lax.dynamic_slice_in_dim(halves, (1 - core) * (count // 2), count // 2, 0)
    other = swap(other)
    first = jnp.where(core == 0, mine, other)
    second = jnp.where(core == 0, other, mine)
    return jnp.concatenate([first[:, None], second[:, None]], 1).reshape(-1, width)


def both(core, mine, other):
    return jnp.concatenate(
        [jnp.where(core == 0, mine, other), jnp.where(core == 0, other, mine)], 0
    )


def plain(matrix, panel):
    core = lax.axis_index("col")
    height, width = panel.shape
    half = height // 2
    panel_half = lax.dynamic_slice_in_dim(panel, core * half, half, 0)
    panel_halves = gather(panel_half)
    flat = panel_halves.reshape(-1, width)
    gram = dot(flat, flat, ((0,), (0,)))
    gram = gram + swap(gram)
    panel_cols = columns(panel_halves, core)
    terms = dot(matrix, panel_cols, precision=THREE)
    mine = lax.dynamic_slice_in_dim(terms, core * half, half, 0)
    other = lax.dynamic_slice_in_dim(terms, (1 - core) * half, half, 0)
    image_half = mine + swap(other)
    image_halves = gather(image_half)

    lower = lax.linalg.cholesky(gram, symmetrize_input=False)
    inverse = lax.linalg.triangular_solve(
        lower, jnp.eye(width, dtype=jnp.float32), left_side=True, lower=True
    )
    basis = dot(panel, inverse, ((1,), (1,)))
    left = dot(2.0 * basis, inverse)
    image = both(core, image_half, swap(image_half))
    image = dot(image, inverse, ((1,), (1,)))

    flat_image = image_halves.reshape(-1, width)
    inner = dot(flat, flat_image, ((0,), (0,)))
    inner = inner + swap(inner)
    image_cols = columns(image_halves, core)
    coupling = dot(dot(inverse, inner), inverse, ((1,), (1,)))
    right = dot(2.0 * image - 4.0 * dot(basis, coupling), inverse)
    updated = matrix - dot(
        jnp.concatenate([left, right], 1),
        jnp.concatenate([image_cols, panel_cols], 1),
        ((1,), (1,)),
        THREE,
    )
    return (updated, basis)


AXES = ("row", "col")
COUNT = len(WALK)


def flat(place, core):
    return WALK[place % COUNT] * 2 + core


ROUND = tuple((flat(i, 0), flat(i + 1, 0)) for i in range(COUNT)) + tuple(
    (flat(i, 1), flat(i - 1, 1)) for i in range(COUNT)
)


def order_table():
    table = np.zeros((COUNT, 2, 4, 2), np.int32)
    for row in range(COUNT):
        place = WALK.index(row)
        for core in range(2):
            away = -1 if core == 0 else 1
            found = []
            for piece in range(COUNT):
                step, first = (piece + 1) // 2, piece % 2 == 1
                origin = WALK[(place + (away if first else -away) * step) % COUNT]
                if origin // 4 == core:
                    found.append((step, piece, origin % 4))
            found.sort()
            for k, (_, piece, block) in enumerate(found):
                table[row, core, k] = piece, block
    return table.reshape(COUNT * 2, 8)


def entry(table, k):
    device = lax.axis_index("row") * 2 + lax.axis_index("col")
    return table[device, 2 * k], table[device, 2 * k + 1]


def split(x):
    high = x.astype(jnp.bfloat16)
    return high, (x - high.astype(jnp.float32)).astype(jnp.bfloat16)


def dot3(a, b, dims=((1,), (0,))):
    one = lambda x, y: lax.dot_general(
        x, y, (dims, ((), ())), preferred_element_type=jnp.float32
    )
    return one(a[0], b[0]) + (one(a[0], b[1]) + one(a[1], b[0]))


TURNED = ((0,), (0,))
ACROSS = ((1,), (1,))


def wide(pieces):
    return jnp.concatenate([x[...] for x in pieces], 1)


def cost(flops, bytes_accessed):
    return pl.CostEstimate(
        flops=int(flops), bytes_accessed=int(bytes_accessed), transcendentals=0
    )


def vmem():
    return pl.BlockSpec(memory_space=pltpu.VMEM)


def anywhere():
    return pl.BlockSpec(memory_space=pl.ANY)


def in_hbm():
    return pl.BlockSpec(memory_space=pltpu.HBM)


def in_smem():
    return pl.BlockSpec(memory_space=pltpu.SMEM)


def block_fetch(matrix, table, k, land, sem, parts=6):
    height, width = land.shape
    at = pl.multiple_of(entry(table, k)[1] * width, width)
    step = height // parts
    for low in range(0, height, step):
        pltpu.make_async_copy(
            matrix.at[pl.ds(low, step), pl.ds(at, width)],
            land.at[pl.ds(low, step)],
            sem,
        ).start()


def params(mib):
    return pltpu.CompilerParams(vmem_limit_bytes=mib * 1024 * 1024)


def in_order(one, two):
    first = lax.axis_index("col") == 0
    one, two = one[...], two[...]
    return jnp.concatenate([jnp.where(first, one, two), jnp.where(first, two, one)], 1)


def inner_kernel(start, count, last, *refs):
    total, pieces, out = refs[:start], refs[start:-1], refs[-1]
    acc = total[0][...] if start else None
    lefts, rights = pieces[:count], pieces[count:]
    for i in range(0, count, 2):
        join = in_order if last and i == count - 2 else lambda *x: wide(x)
        left = join(*lefts[i : i + 2])
        right = join(*rights[i : i + 2]) if rights else left
        if rights:
            term = dot3(split(left), split(right), TURNED)
        else:
            term = dot(left, right, TURNED)
        acc = term if acc is None else acc + term
    out[...] = acc


def inner(total, lefts, rights=(), last=False):
    lefts = [x for pair in lefts for x in pair]
    rights = [x for pair in rights for x in pair]
    width = 2 * lefts[0].shape[1]
    rows = sum(x.shape[0] for x in lefts[::2])
    args = ([] if total is None else [total]) + lefts + rights
    return pl.pallas_call(
        functools.partial(
            inner_kernel, 0 if total is None else 1, len(lefts), last
        ),
        out_shape=jax.ShapeDtypeStruct((width, width), jnp.float32),
        in_specs=[vmem()] * len(args),
        out_specs=vmem(),
        compiler_params=params(6),
        cost_estimate=cost(12 * rows * width * width, 8 * rows * width),
    )(*args)


def fetch(pieces, which, lands, sems):
    core = lax.axis_index("col")
    for index, pair in enumerate(pieces):
        turns = ((0, 1), (1, 0)) if index == COUNT - 1 else ((0, 1),)
        for turn, sides in enumerate(turns):
            here = which == index
            if len(turns) > 1:
                here = jnp.logical_and(here, core == turn)

            @pl.when(here)
            def _():
                for source, side in enumerate(sides):
                    pltpu.make_async_copy(
                        pair[source], lands[side], sems.at[side]
                    ).start()


def pick(pieces, which, land):
    for index, pair in enumerate(pieces):
        join = in_order if index == COUNT - 1 else lambda *x: wide(x)

        @pl.when(which == index)
        def _():
            land[...] = join(*pair)


def landed(lands, sems):
    for side in range(2):
        pltpu.make_async_copy(lands[side], lands[side], sems.at[side]).wait()


def pair_up(refs):
    return [refs[i : i + 2] for i in range(0, len(refs), 2)]


def load_kernel(first, table, matrix, *refs):
    *outs, sems = refs
    for k, out in enumerate(outs):
        block_fetch(matrix, table, first + k, out, sems.at[k])
    for k, out in enumerate(outs):
        pltpu.make_async_copy(out, out, sems.at[k]).wait()


def load(table, matrix, first, blocks):
    height = matrix.shape[0]
    columns = blocks * height
    return pl.pallas_call(
        functools.partial(load_kernel, first),
        in_specs=[in_smem(), in_hbm()],
        out_specs=[vmem()] * blocks,
        out_shape=[jax.ShapeDtypeStruct((height, height), jnp.float32)] * blocks,
        scratch_shapes=[pltpu.SemaphoreType.DMA((blocks,))],
        compiler_params=params(46),
        cost_estimate=cost(height * columns, 8 * height * columns),
    )(table, matrix)


def term_kernel(first, blocks, count, *refs):
    table, matrix, refs = refs[0], refs[1 : 1 + blocks], refs[1 + blocks :]
    start = 2 if first else 0
    total, refs = refs[:start], refs[start:]
    pieces = pair_up(refs[:count])
    out0, out1, kept_high, kept_low, land = refs[count:]
    height, middle = out0.shape
    acc = wide(total) if start else None
    for k in range(blocks):
        left = split(matrix[k][...])
        pick(pieces, entry(table, first + k)[0], land)
        right = split(land[...])
        rows = slice(k * height, k * height + height)
        kept_high[rows], kept_low[rows] = right
        term = dot3(left, right)
        acc = term if acc is None else acc + term
    out0[...], out1[...] = acc[:, :middle], acc[:, middle:]


def terms(table, matrix, total, pieces, first):
    blocks, height = len(matrix), matrix[0].shape[0]
    middle = pieces[0][0].shape[1]
    width = 2 * middle
    flat_pieces = [x for pair in pieces for x in pair]
    begin = [] if total is None else list(total)
    *total, high, low = pl.pallas_call(
        functools.partial(term_kernel, first, blocks, len(flat_pieces)),
        in_specs=[in_smem()]
        + [vmem()] * (blocks + len(begin) + len(flat_pieces)),
        out_specs=[vmem()] * 4,
        scratch_shapes=[pltpu.VMEM((height, width), jnp.float32)],
        out_shape=[jax.ShapeDtypeStruct((height, middle), jnp.float32)] * 2
        + [jax.ShapeDtypeStruct((blocks * height, width), jnp.bfloat16)] * 2,
        compiler_params=params(11),
        cost_estimate=cost(
            6 * blocks * height * height * width, 4 * blocks * height * height
        ),
    )(table, *matrix, *begin, *flat_pieces)
    return total, (high, low)


def factor(out, work, rows, tops, block=64, group=8):
    size = out.shape[0]
    index = lax.broadcasted_iota(jnp.int32, (block, 128), 0)
    for top in tops:
        low = top // 128 * 128
        high = low + 128
        strip = jnp.concatenate(
            [work[top : top + block, low:], rows[top : top + block, :high]], 1
        )
        tiles = strip.shape[1] // 128
        spread = lambda x: jnp.concatenate([x] * tiles, 1)
        pivots = jnp.ones((block, 128), jnp.float32)
        for j in range(0, block, group):
            at = top - low + j
            some = range(group)
            down = [
                jnp.broadcast_to(strip[:, at + m : at + m + 1], (block, 128))
                for m in some
            ]
            along = [strip[j + m : j + m + 1, :] for m in some]
            cell = {
                (m, i): jnp.broadcast_to(
                    strip[j + m : j + m + 1, at + i : at + i + 1], (1, 128)
                )
                for m in some
                for i in range(m, group)
            }
            for m in some:
                over = 1.0 / cell[m, m]
                pivots = jnp.where(index == j + m, cell[m, m], pivots)
                row = along[m] * spread(over)
                strip = strip - spread(jnp.where(index > j + m, down[m], 0.0)) * row
                for i in range(m + 1, group):
                    ratio = cell[m, i] * over
                    along[i] = along[i] - spread(cell[m, i]) * row
                    down[i] = down[i] - down[m] * ratio
                    for h in range(i, group):
                        cell[i, h] = cell[i, h] - cell[m, h] * ratio
        strip = strip * spread(lax.rsqrt(pivots))
        out[top : top + block, :high] = strip[:, size - low :]
        if high < size:
            out[top : top + block, high:] = jnp.zeros(
                (block, size - high), jnp.float32
            )
        after = top + block
        if after < size:
            base = after // 128 * 128
            update = dot(strip[:, base - low : size - low], strip[:, base - low :], TURNED)
            update = update[after - base :]
            work[after:, base:] -= update[:, : size - base]
            rows[after:, :high] -= update[:, size - base :]


def first_kernel(gram, out, work, rows):
    size = gram.shape[0]
    work[...] = gram[...]
    line = lax.broadcasted_iota(jnp.int32, (size, size), 0)
    lane = lax.broadcasted_iota(jnp.int32, (size, size), 1)
    rows[...] = jnp.where(line == lane, 1.0, 0.0).astype(jnp.float32)
    factor(out, work, rows, range(0, size // 2, 64))
    out[size // 2 :, :] = jnp.zeros((size // 2, size), jnp.float32)


def second_kernel(begun, work_in, rows_in, out, work, rows):
    size = out.shape[0]
    work[...] = work_in[...]
    rows[...] = rows_in[...]
    out[...] = begun[...]
    factor(out, work, rows, range(size // 2, size, 64))


def factor_call(kernel, args, scratch):
    size = args[0].shape[0]
    shape = (size, size)
    outs = 1 if scratch else 3
    return pl.pallas_call(
        kernel,
        out_shape=[jax.ShapeDtypeStruct(shape, jnp.float32)] * outs,
        in_specs=[vmem()] * len(args),
        out_specs=[vmem()] * outs,
        scratch_shapes=[pltpu.VMEM(shape, jnp.float32)] * scratch,
        compiler_params=params(4),
        cost_estimate=cost(4e9, 4 * size * size),
    )(*args)


def left_kernel(panel, image0, image1, inverse, basis, left, right):
    inv = inverse[...]
    rows = dot(panel[...], inv, ACROSS)
    basis[...] = rows
    inv = split(inv)
    left[...] = dot3(split(2.0 * rows), inv)
    image = dot3(split(wide((image0, image1))), inv, ACROSS)
    right[...] = dot3(split(2.0 * image), inv)


def lefts(panel, images, inverse):
    height, width = panel.shape
    return pl.pallas_call(
        left_kernel,
        out_shape=[jax.ShapeDtypeStruct((height, width), jnp.float32)] * 3,
        in_specs=[vmem()] * 4,
        out_specs=[vmem()] * 3,
        compiler_params=params(8),
        cost_estimate=cost(48 * height * width * width, 20 * height * width),
    )(panel, *images, inverse)


def before_kernel(blocks, count, *refs):
    table, left, matrix, refs = refs[0], refs[1], refs[2 : 2 + blocks], refs[2 + blocks :]
    pieces, (out, land) = pair_up(refs[:count]), refs[count:]
    one = split(left[...])
    for k in range(blocks):
        pick(pieces, entry(table, k)[0], land)
        right = split(land[...])
        out[k] = matrix[k][...] - dot3(one, right, ACROSS)


def before(table, matrix, left, pieces):
    blocks = len(matrix)
    height, width = left.shape
    flat_pieces = [x for pair in pieces for x in pair]
    return pl.pallas_call(
        functools.partial(before_kernel, blocks, len(flat_pieces)),
        in_specs=[in_smem()] + [vmem()] * (1 + blocks + len(flat_pieces)),
        out_specs=vmem(),
        scratch_shapes=[pltpu.VMEM((height, width), jnp.float32)],
        out_shape=jax.ShapeDtypeStruct((blocks, height, height), jnp.float32),
        compiler_params=params(10),
        cost_estimate=cost(
            6 * blocks * height * height * width, 8 * blocks * height * height
        ),
    )(table, left, *matrix, *flat_pieces)


def update_kernel(last, *refs):
    table, matrix, early, total, inverse, basis, left, right = refs[:8]
    kept, pieces = pair_up(refs[8:14]), pair_up(refs[14:30])
    panel_last, image_last = refs[30:32], pieces[-1]
    out, held, third, land, out_sems = refs[32:]
    height = left.shape[0]
    pick(pieces, entry(table, last)[0], land)
    acc = total[...] + dot3(
        split(in_order(*panel_last)), split(in_order(*image_last)), TURNED
    )
    inv = inverse[...]
    coupling = dot(dot(inv, acc), inv, ACROSS)
    y = right[...] - dot3(split(basis[...]), split(dot(4.0 * coupling, inv)))
    y = split(y)
    third[...] = matrix[...] - dot3(
        split(left[...]), split(land[...]), ACROSS
    )
    slots, width, count = held.shape[0], held.shape[2], 0
    writes = []
    for k in range(last + 1):
        high, low = kept[min(k, 1) if k < last else 2]
        top = 0 if k in (0, last) else (k - 1) * height
        at = entry(table, k)[1] * height
        for low_column in range(0, height, width):
            rows = slice(top + low_column, top + low_column + width)
            columns = slice(low_column, low_column + width)
            term = dot3(y, (high[rows], low[rows]), ACROSS)
            begin = early[k, :, columns] if k < last else third[:, columns]
            slot = count % slots
            if count >= slots:
                writes[count - slots].wait()
            held[slot] = begin - term
            where = pl.ds(pl.multiple_of(at + low_column, width), width)
            writes.append(
                pltpu.make_async_copy(held.at[slot], out.at[:, where], out_sems.at[slot])
            )
            writes[-1].start()
            count += 1
    for write in writes[-slots:]:
        write.wait()


def update(table, matrix, early, total, inverse, basis, left, right, kept, pieces, opposite):
    height, width = basis.shape
    blocks = early.shape[0] + 1
    columns = blocks * height
    flat_pieces = [x for pair in pieces for x in pair]
    return pl.pallas_call(
        functools.partial(update_kernel, blocks - 1),
        in_specs=[in_smem()]
        + [vmem()] * (15 + len(flat_pieces)),
        out_specs=in_hbm(),
        scratch_shapes=[
            pltpu.VMEM((6, height, width), jnp.float32),
            pltpu.VMEM((height, height), jnp.float32),
            pltpu.VMEM((height, width), jnp.float32),
            pltpu.SemaphoreType.DMA((6,)),
        ],
        out_shape=jax.ShapeDtypeStruct((height, columns), jnp.float32),
        compiler_params=params(18),
        cost_estimate=cost(12 * height * columns * width, 8 * height * columns),
    )(
        table, matrix, early, total, inverse, basis, left, right,
        *(x for pair in kept for x in pair),
        *flat_pieces, *opposite,
    )


def hop(x):
    return lax.ppermute(x, AXES, ROUND)


def swapped(pair):
    return tuple(swap(x) for x in pair)


def after(x, *others):
    return lax.optimization_barrier((x, *others))[0]


def ring(matrix, panel):
    panel, first = lax.optimization_barrier((panel, lax.axis_index("col") == 0))
    table = jnp.asarray(order_table())
    middle = panel.shape[1] // 2

    own = (panel[:, :middle], panel[:, middle:])
    early_blocks = load(table, matrix, 0, 2)
    late_blocks = load(table, matrix, 2, 2)
    matrix = (*early_blocks, *late_blocks)
    a1 = (hop(own[0]), hop(own[1]))
    b1 = (swap(after(a1[0], *early_blocks)), swap(a1[1]))
    gram = inner(None, [own, a1, b1])
    a2 = (hop(a1[0]), hop(a1[1]))
    b2 = (swap(after(a2[0], *late_blocks)), swap(a2[1]))
    a3 = (hop(after(a2[0], gram)), hop(a2[1]))
    b3 = swapped(a3)
    gram = inner(gram, [a2, b2])
    image, kept = terms(table, matrix[:1], None, [own, a1, b1, a2, b2], 0)
    kepts = [kept]
    one = hop(jnp.where(first, a3[0], after(a3[1], gram, image[0])))
    panels = [own, a1, b1, a2, b2, a3, b3]
    image, kept = terms(table, matrix[1:3], image, panels, 1)
    kepts.append(kept)
    opposite = (one, swap(after(one, image[0])))
    image, kept = terms(table, matrix[3:], image, [*panels, opposite], 3)
    kepts.append(kept)

    image = tuple(x + swap(x) for x in image)
    gram = inner(gram, [a3, b3, opposite], last=True)
    c1 = (hop(after(image[0], gram)), hop(image[1]))
    d1 = swapped(c1)
    begun = factor_call(first_kernel, [gram], 0)
    c2 = (hop(after(c1[0], begun[0])), hop(c1[1]))
    (inverse,) = factor_call(second_kernel, begun, 2)
    basis, left, right = lefts(panel, image, inverse)
    total = inner(None, panels[:3], [image, c1, d1])
    c3 = (hop(after(c2[0], inverse)), hop(c2[1]))
    d2 = (swap(after(c2[0], left)), swap(after(c2[1], total)))
    d3 = swapped(c3)
    one = hop(jnp.where(first, c3[0], c3[1]))
    images = [image, c1, d1, c2, d2, c3, d3]
    total = inner(total, panels[3:], images[3:])
    early = before(table, matrix[:3], left, images)
    last = (one, swap(after(one, total, early)))
    updated = update(
        table, matrix[3], early, total, inverse, basis, left, right, kepts,
        [*images, last], opposite,
    )
    return (updated, basis)


def solution(mesh):
    count, cores = mesh.shape["row"], mesh.shape["col"]
    return jax.shard_map(
        ring if (count, cores) == (len(WALK), 2) else plain,
        mesh=mesh,
        in_specs=(P(("grp", "row"), "col"), P(("grp", "row"), None)),
        out_specs=(P(("grp", "row"), "col"), P(("grp", "row"), None)),
        check_vma=False,
    )
```

```python
import functools

import jax
import jax.numpy as jnp
import numpy as np
from jax import lax
from jax.experimental import pallas as pl
from jax.experimental.pallas import tpu as pltpu
from jax.sharding import PartitionSpec as P

WALK = (0, 2, 4, 6, 7, 5, 3, 1)
FULL = lax.Precision.HIGHEST
THREE = lax.Precision.HIGH


def dot(a, b, dims=((1,), (0,)), precision=FULL):
    return lax.dot_general(
        a, b, (dims, ((), ())), precision=precision, preferred_element_type=jnp.float32
    )


def swap(x):
    return lax.ppermute(x, "col", ((0, 1), (1, 0)))


def gather(part):
    return lax.all_gather(part, "row", axis=0)


def columns(halves, core):
    count, height, width = halves.shape
    mine = lax.dynamic_slice_in_dim(halves, core * (count // 2), count // 2, 0)
    other = lax.dynamic_slice_in_dim(halves, (1 - core) * (count // 2), count // 2, 0)
    other = swap(other)
    first = jnp.where(core == 0, mine, other)
    second = jnp.where(core == 0, other, mine)
    return jnp.concatenate([first[:, None], second[:, None]], 1).reshape(-1, width)


def both(core, mine, other):
    return jnp.concatenate(
        [jnp.where(core == 0, mine, other), jnp.where(core == 0, other, mine)], 0
    )


def plain(matrix, panel):
    core = lax.axis_index("col")
    height, width = panel.shape
    half = height // 2
    panel_half = lax.dynamic_slice_in_dim(panel, core * half, half, 0)
    panel_halves = gather(panel_half)
    flat = panel_halves.reshape(-1, width)
    gram = dot(flat, flat, ((0,), (0,)))
    gram = gram + swap(gram)
    panel_cols = columns(panel_halves, core)
    terms = dot(matrix, panel_cols, precision=THREE)
    mine = lax.dynamic_slice_in_dim(terms, core * half, half, 0)
    other = lax.dynamic_slice_in_dim(terms, (1 - core) * half, half, 0)
    image_half = mine + swap(other)
    image_halves = gather(image_half)

    lower = lax.linalg.cholesky(gram, symmetrize_input=False)
    inverse = lax.linalg.triangular_solve(
        lower, jnp.eye(width, dtype=jnp.float32), left_side=True, lower=True
    )
    basis = dot(panel, inverse, ((1,), (1,)))
    left = dot(2.0 * basis, inverse)
    image = both(core, image_half, swap(image_half))
    image = dot(image, inverse, ((1,), (1,)))

    flat_image = image_halves.reshape(-1, width)
    inner = dot(flat, flat_image, ((0,), (0,)))
    inner = inner + swap(inner)
    image_cols = columns(image_halves, core)
    coupling = dot(dot(inverse, inner), inverse, ((1,), (1,)))
    right = dot(2.0 * image - 4.0 * dot(basis, coupling), inverse)
    updated = matrix - dot(
        jnp.concatenate([left, right], 1),
        jnp.concatenate([image_cols, panel_cols], 1),
        ((1,), (1,)),
        THREE,
    )
    return (updated, basis)


AXES = ("row", "col")
COUNT = len(WALK)


def flat(place, core):
    return WALK[place % COUNT] * 2 + core


ROUND = tuple((flat(i, 0), flat(i + 1, 0)) for i in range(COUNT)) + tuple(
    (flat(i, 1), flat(i - 1, 1)) for i in range(COUNT)
)


def order_table():
    table = np.zeros((COUNT, 2, 4, 2), np.int32)
    for row in range(COUNT):
        place = WALK.index(row)
        for core in range(2):
            away = -1 if core == 0 else 1
            found = []
            for piece in range(COUNT):
                step, first = (piece + 1) // 2, piece % 2 == 1
                origin = WALK[(place + (away if first else -away) * step) % COUNT]
                if origin // 4 == core:
                    found.append((step, piece, origin % 4))
            found.sort()
            for k, (_, piece, block) in enumerate(found):
                table[row, core, k] = piece, block
    return table.reshape(COUNT * 2, 8)


def entry(table, k):
    device = lax.axis_index("row") * 2 + lax.axis_index("col")
    return table[device, 2 * k], table[device, 2 * k + 1]


def split(x):
    high = x.astype(jnp.bfloat16)
    return high, (x - high.astype(jnp.float32)).astype(jnp.bfloat16)


def dot3(a, b, dims=((1,), (0,))):
    one = lambda x, y: lax.dot_general(
        x, y, (dims, ((), ())), preferred_element_type=jnp.float32
    )
    return one(a[0], b[0]) + (one(a[0], b[1]) + one(a[1], b[0]))


TURNED = ((0,), (0,))
ACROSS = ((1,), (1,))


def wide(pieces):
    return jnp.concatenate([x[...] for x in pieces], 1)


def cost(flops, bytes_accessed):
    return pl.CostEstimate(
        flops=int(flops), bytes_accessed=int(bytes_accessed), transcendentals=0
    )


def vmem():
    return pl.BlockSpec(memory_space=pltpu.VMEM)


def anywhere():
    return pl.BlockSpec(memory_space=pl.ANY)


def in_hbm():
    return pl.BlockSpec(memory_space=pltpu.HBM)


def in_smem():
    return pl.BlockSpec(memory_space=pltpu.SMEM)


def block_fetch(matrix, table, k, land, sem, parts=6):
    height, width = land.shape
    at = pl.multiple_of(entry(table, k)[1] * width, width)
    step = height // parts
    for low in range(0, height, step):
        pltpu.make_async_copy(
            matrix.at[pl.ds(low, step), pl.ds(at, width)],
            land.at[pl.ds(low, step)],
            sem,
        ).start()


def params(mib):
    return pltpu.CompilerParams(vmem_limit_bytes=mib * 1024 * 1024)


def in_order(one, two):
    first = lax.axis_index("col") == 0
    one, two = one[...], two[...]
    return jnp.concatenate([jnp.where(first, one, two), jnp.where(first, two, one)], 1)


def inner_kernel(start, count, last, *refs):
    total, pieces, out = refs[:start], refs[start:-1], refs[-1]
    acc = total[0][...] if start else None
    lefts, rights = pieces[:count], pieces[count:]
    for i in range(0, count, 2):
        join = in_order if last and i == count - 2 else lambda *x: wide(x)
        left = join(*lefts[i : i + 2])
        right = join(*rights[i : i + 2]) if rights else left
        if rights:
            term = dot3(split(left), split(right), TURNED)
        else:
            term = dot(left, right, TURNED)
        acc = term if acc is None else acc + term
    out[...] = acc


def inner(total, lefts, rights=(), last=False):
    lefts = [x for pair in lefts for x in pair]
    rights = [x for pair in rights for x in pair]
    width = 2 * lefts[0].shape[1]
    rows = sum(x.shape[0] for x in lefts[::2])
    args = ([] if total is None else [total]) + lefts + rights
    return pl.pallas_call(
        functools.partial(
            inner_kernel, 0 if total is None else 1, len(lefts), last
        ),
        out_shape=jax.ShapeDtypeStruct((width, width), jnp.float32),
        in_specs=[vmem()] * len(args),
        out_specs=vmem(),
        compiler_params=params(6),
        cost_estimate=cost(12 * rows * width * width, 8 * rows * width),
    )(*args)


def fetch(pieces, which, lands, sems):
    core = lax.axis_index("col")
    for index, pair in enumerate(pieces):
        turns = ((0, 1), (1, 0)) if index == COUNT - 1 else ((0, 1),)
        for turn, sides in enumerate(turns):
            here = which == index
            if len(turns) > 1:
                here = jnp.logical_and(here, core == turn)

            @pl.when(here)
            def _():
                for source, side in enumerate(sides):
                    pltpu.make_async_copy(
                        pair[source], lands[side], sems.at[side]
                    ).start()


def pick(pieces, which, land):
    for index, pair in enumerate(pieces):
        join = in_order if index == COUNT - 1 else lambda *x: wide(x)

        @pl.when(which == index)
        def _():
            land[...] = join(*pair)


def landed(lands, sems):
    for side in range(2):
        pltpu.make_async_copy(lands[side], lands[side], sems.at[side]).wait()


def pair_up(refs):
    return [refs[i : i + 2] for i in range(0, len(refs), 2)]


def load_kernel(first, table, matrix, *refs):
    *outs, sems = refs
    for k, out in enumerate(outs):
        block_fetch(matrix, table, first + k, out, sems.at[k])
    for k, out in enumerate(outs):
        pltpu.make_async_copy(out, out, sems.at[k]).wait()


def load(table, matrix, first, blocks):
    height = matrix.shape[0]
    columns = blocks * height
    return pl.pallas_call(
        functools.partial(load_kernel, first),
        in_specs=[in_smem(), in_hbm()],
        out_specs=[vmem()] * blocks,
        out_shape=[jax.ShapeDtypeStruct((height, height), jnp.float32)] * blocks,
        scratch_shapes=[pltpu.SemaphoreType.DMA((blocks,))],
        compiler_params=params(46),
        cost_estimate=cost(height * columns, 8 * height * columns),
    )(table, matrix)


def term_kernel(first, blocks, count, *refs):
    table, matrix, refs = refs[0], refs[1 : 1 + blocks], refs[1 + blocks :]
    start = 2 if first else 0
    total, refs = refs[:start], refs[start:]
    pieces = pair_up(refs[:count])
    out0, out1, kept_high, kept_low, land = refs[count:]
    height, middle = out0.shape
    acc = wide(total) if start else None
    for k in range(blocks):
        left = split(matrix[k][...])
        pick(pieces, entry(table, first + k)[0], land)
        right = split(land[...])
        rows = slice(k * height, k * height + height)
        kept_high[rows], kept_low[rows] = right
        term = dot3(left, right)
        acc = term if acc is None else acc + term
    out0[...], out1[...] = acc[:, :middle], acc[:, middle:]


def terms(table, matrix, total, pieces, first):
    blocks, height = len(matrix), matrix[0].shape[0]
    middle = pieces[0][0].shape[1]
    width = 2 * middle
    flat_pieces = [x for pair in pieces for x in pair]
    begin = [] if total is None else list(total)
    *total, high, low = pl.pallas_call(
        functools.partial(term_kernel, first, blocks, len(flat_pieces)),
        in_specs=[in_smem()]
        + [vmem()] * (blocks + len(begin) + len(flat_pieces)),
        out_specs=[vmem()] * 4,
        scratch_shapes=[pltpu.VMEM((height, width), jnp.float32)],
        out_shape=[jax.ShapeDtypeStruct((height, middle), jnp.float32)] * 2
        + [jax.ShapeDtypeStruct((blocks * height, width), jnp.bfloat16)] * 2,
        compiler_params=params(11),
        cost_estimate=cost(
            6 * blocks * height * height * width, 4 * blocks * height * height
        ),
    )(table, *matrix, *begin, *flat_pieces)
    return total, (high, low)


def factor(out, work, rows, tops, block=64, group=8):
    size = out.shape[0]
    index = lax.broadcasted_iota(jnp.int32, (block, 128), 0)
    for top in tops:
        low = top // 128 * 128
        high = low + 128
        strip = jnp.concatenate(
            [work[top : top + block, low:], rows[top : top + block, :high]], 1
        )
        tiles = strip.shape[1] // 128
        spread = lambda x: jnp.concatenate([x] * tiles, 1)
        pivots = jnp.ones((block, 128), jnp.float32)
        for j in range(0, block, group):
            at = top - low + j
            some = range(group)
            down = [
                jnp.broadcast_to(strip[:, at + m : at + m + 1], (block, 128))
                for m in some
            ]
            along = [strip[j + m : j + m + 1, :] for m in some]
            cell = {
                (m, i): jnp.broadcast_to(
                    strip[j + m : j + m + 1, at + i : at + i + 1], (1, 128)
                )
                for m in some
                for i in range(m, group)
            }
            for m in some:
                over = 1.0 / cell[m, m]
                pivots = jnp.where(index == j + m, cell[m, m], pivots)
                row = along[m] * spread(over)
                strip = strip - spread(jnp.where(index > j + m, down[m], 0.0)) * row
                for i in range(m + 1, group):
                    ratio = cell[m, i] * over
                    along[i] = along[i] - spread(cell[m, i]) * row
                    down[i] = down[i] - down[m] * ratio
                    for h in range(i, group):
                        cell[i, h] = cell[i, h] - cell[m, h] * ratio
        strip = strip * spread(lax.rsqrt(pivots))
        out[top : top + block, :high] = strip[:, size - low :]
        if high < size:
            out[top : top + block, high:] = jnp.zeros(
                (block, size - high), jnp.float32
            )
        after = top + block
        if after < size:
            base = after // 128 * 128
            update = dot(strip[:, base - low : size - low], strip[:, base - low :], TURNED)
            update = update[after - base :]
            work[after:, base:] -= update[:, : size - base]
            rows[after:, :high] -= update[:, size - base :]


def first_kernel(gram, out, work, rows):
    size = gram.shape[0]
    work[...] = gram[...]
    line = lax.broadcasted_iota(jnp.int32, (size, size), 0)
    lane = lax.broadcasted_iota(jnp.int32, (size, size), 1)
    rows[...] = jnp.where(line == lane, 1.0, 0.0).astype(jnp.float32)
    factor(out, work, rows, range(0, size // 2, 64))
    out[size // 2 :, :] = jnp.zeros((size // 2, size), jnp.float32)


def second_kernel(begun, work_in, rows_in, out, work, rows):
    size = out.shape[0]
    work[...] = work_in[...]
    rows[...] = rows_in[...]
    out[...] = begun[...]
    factor(out, work, rows, range(size // 2, size, 64))


def factor_call(kernel, args, scratch):
    size = args[0].shape[0]
    shape = (size, size)
    outs = 1 if scratch else 3
    return pl.pallas_call(
        kernel,
        out_shape=[jax.ShapeDtypeStruct(shape, jnp.float32)] * outs,
        in_specs=[vmem()] * len(args),
        out_specs=[vmem()] * outs,
        scratch_shapes=[pltpu.VMEM(shape, jnp.float32)] * scratch,
        compiler_params=params(4),
        cost_estimate=cost(4e9, 4 * size * size),
    )(*args)


def left_kernel(panel, image0, image1, inverse, basis, left, right, normal):
    inv = inverse[...]
    rows = dot(panel[...], inv, ACROSS)
    basis[...] = rows
    normal[...] = dot(4.0 * inv, inv, TURNED)
    inv = split(inv)
    left[...] = dot3(split(2.0 * rows), inv)
    image = dot3(split(wide((image0, image1))), inv, ACROSS)
    right[...] = dot3(split(2.0 * image), inv)


def lefts(panel, images, inverse):
    height, width = panel.shape
    return pl.pallas_call(
        left_kernel,
        out_shape=[jax.ShapeDtypeStruct((height, width), jnp.float32)] * 3
        + [jax.ShapeDtypeStruct((width, width), jnp.float32)],
        in_specs=[vmem()] * 4,
        out_specs=[vmem()] * 4,
        compiler_params=params(8),
        cost_estimate=cost(48 * height * width * width, 20 * height * width),
    )(panel, *images, inverse)


def before_kernel(blocks, count, *refs):
    table, left, matrix, refs = refs[0], refs[1], refs[2 : 2 + blocks], refs[2 + blocks :]
    pieces, (out, land) = pair_up(refs[:count]), refs[count:]
    one = split(left[...])
    for k in range(blocks):
        pick(pieces, entry(table, k)[0], land)
        right = split(land[...])
        out[k] = matrix[k][...] - dot3(one, right, ACROSS)


def before(table, matrix, left, pieces):
    blocks = len(matrix)
    height, width = left.shape
    flat_pieces = [x for pair in pieces for x in pair]
    return pl.pallas_call(
        functools.partial(before_kernel, blocks, len(flat_pieces)),
        in_specs=[in_smem()] + [vmem()] * (1 + blocks + len(flat_pieces)),
        out_specs=vmem(),
        scratch_shapes=[pltpu.VMEM((height, width), jnp.float32)],
        out_shape=jax.ShapeDtypeStruct((blocks, height, height), jnp.float32),
        compiler_params=params(10),
        cost_estimate=cost(
            6 * blocks * height * height * width, 8 * blocks * height * height
        ),
    )(table, left, *matrix, *flat_pieces)


def update_kernel(last, *refs):
    table, matrix, early, total, inverse, normal, basis, left, right = refs[:9]
    kept, pieces = pair_up(refs[9:15]), pair_up(refs[15:31])
    panel_last, image_last = refs[31:33], pieces[-1]
    out, held, third, land, out_sems = refs[33:]
    height = left.shape[0]
    pick(pieces, entry(table, last)[0], land)
    acc = total[...] + dot3(
        split(in_order(*panel_last)), split(in_order(*image_last)), TURNED
    )
    middle = dot(inverse[...], dot(acc, normal[...]))
    y = right[...] - dot3(split(basis[...]), split(middle))
    y = split(y)
    third[...] = matrix[...] - dot3(
        split(left[...]), split(land[...]), ACROSS
    )
    slots, width, count = held.shape[0], held.shape[2], 0
    writes = []
    for k in range(last + 1):
        high, low = kept[min(k, 1) if k < last else 2]
        top = 0 if k in (0, last) else (k - 1) * height
        at = entry(table, k)[1] * height
        for low_column in range(0, height, width):
            rows = slice(top + low_column, top + low_column + width)
            columns = slice(low_column, low_column + width)
            term = dot3(y, (high[rows], low[rows]), ACROSS)
            begin = early[k, :, columns] if k < last else third[:, columns]
            slot = count % slots
            if count >= slots:
                writes[count - slots].wait()
            held[slot] = begin - term
            where = pl.ds(pl.multiple_of(at + low_column, width), width)
            writes.append(
                pltpu.make_async_copy(held.at[slot], out.at[:, where], out_sems.at[slot])
            )
            writes[-1].start()
            count += 1
    for write in writes[-slots:]:
        write.wait()


def update(table, matrix, early, total, inverse, normal, basis, left, right, kept, pieces, opposite):
    height, width = basis.shape
    blocks = early.shape[0] + 1
    columns = blocks * height
    flat_pieces = [x for pair in pieces for x in pair]
    return pl.pallas_call(
        functools.partial(update_kernel, blocks - 1),
        in_specs=[in_smem()]
        + [vmem()] * (16 + len(flat_pieces)),
        out_specs=in_hbm(),
        scratch_shapes=[
            pltpu.VMEM((6, height, width), jnp.float32),
            pltpu.VMEM((height, height), jnp.float32),
            pltpu.VMEM((height, width), jnp.float32),
            pltpu.SemaphoreType.DMA((6,)),
        ],
        out_shape=jax.ShapeDtypeStruct((height, columns), jnp.float32),
        compiler_params=params(18),
        cost_estimate=cost(12 * height * columns * width, 8 * height * columns),
    )(
        table, matrix, early, total, inverse, normal, basis, left, right,
        *(x for pair in kept for x in pair),
        *flat_pieces, *opposite,
    )


def hop(x):
    return lax.ppermute(x, AXES, ROUND)


def swapped(pair):
    return tuple(swap(x) for x in pair)


def after(x, *others):
    return lax.optimization_barrier((x, *others))[0]


def ring(matrix, panel):
    panel, first = lax.optimization_barrier((panel, lax.axis_index("col") == 0))
    table = jnp.asarray(order_table())
    middle = panel.shape[1] // 2

    own = (panel[:, :middle], panel[:, middle:])
    early_blocks = load(table, matrix, 0, 2)
    late_blocks = load(table, matrix, 2, 2)
    matrix = (*early_blocks, *late_blocks)
    a1 = (hop(own[0]), hop(own[1]))
    b1 = (swap(after(a1[0], *early_blocks)), swap(a1[1]))
    gram = inner(None, [own, a1, b1])
    a2 = (hop(a1[0]), hop(a1[1]))
    b2 = swapped(a2)
    a3 = (hop(after(a2[0], gram)), hop(a2[1]))
    b3 = swapped(a3)
    gram = inner(gram, [a2, b2])
    image, kept = terms(table, [after(matrix[0], *late_blocks)], None, [own, a1, b1, a2, b2], 0)
    kepts = [kept]
    one = hop(jnp.where(first, a3[0], after(a3[1], image[0])))
    panels = [own, a1, b1, a2, b2, a3, b3]
    image, kept = terms(table, matrix[1:3], image, panels, 1)
    kepts.append(kept)
    opposite = (one, swap(after(one, image[0])))
    image, kept = terms(table, [after(matrix[3], gram)], image, [*panels, opposite], 3)
    kepts.append(kept)

    image = tuple(x + swap(x) for x in image)
    gram = inner(gram, [a3, b3, opposite], last=True)
    c1 = (hop(after(image[0], gram)), hop(image[1]))
    d1 = swapped(c1)
    begun = factor_call(first_kernel, [gram], 0)
    c2 = (hop(after(c1[0], begun[0])), hop(c1[1]))
    (inverse,) = factor_call(second_kernel, begun, 2)
    basis, left, right, normal = lefts(panel, image, inverse)
    total = inner(None, panels[:3], [image, c1, d1])
    c3 = (hop(after(c2[0], inverse)), hop(c2[1]))
    d2 = (swap(after(c2[0], left)), swap(after(c2[1], total)))
    d3 = swapped(c3)
    one = hop(jnp.where(first, c3[0], c3[1]))
    images = [image, c1, d1, c2, d2, c3, d3]
    total = inner(total, panels[3:], images[3:])
    early = before(table, matrix[:3], left, images)
    last = (one, swap(after(one, early)))
    updated = update(
        table, matrix[3], early, total, inverse, normal, basis, left, right, kepts,
        [*images, last], opposite,
    )
    return (updated, basis)


def solution(mesh):
    count, cores = mesh.shape["row"], mesh.shape["col"]
    return jax.shard_map(
        ring if (count, cores) == (len(WALK), 2) else plain,
        mesh=mesh,
        in_specs=(P(("grp", "row"), "col"), P(("grp", "row"), None)),
        out_specs=(P(("grp", "row"), "col"), P(("grp", "row"), None)),
        check_vma=False,
    )
```

```python
import functools

import jax
import jax.numpy as jnp
import numpy as np
from jax import lax
from jax.experimental import pallas as pl
from jax.experimental.pallas import tpu as pltpu
from jax.sharding import PartitionSpec as P

WALK = (0, 2, 4, 6, 7, 5, 3, 1)
FULL = lax.Precision.HIGHEST
THREE = lax.Precision.HIGH


def dot(a, b, dims=((1,), (0,)), precision=FULL):
    return lax.dot_general(
        a, b, (dims, ((), ())), precision=precision, preferred_element_type=jnp.float32
    )


def swap(x):
    return lax.ppermute(x, "col", ((0, 1), (1, 0)))


def gather(part):
    return lax.all_gather(part, "row", axis=0)


def columns(halves, core):
    count, height, width = halves.shape
    mine = lax.dynamic_slice_in_dim(halves, core * (count // 2), count // 2, 0)
    other = lax.dynamic_slice_in_dim(halves, (1 - core) * (count // 2), count // 2, 0)
    other = swap(other)
    first = jnp.where(core == 0, mine, other)
    second = jnp.where(core == 0, other, mine)
    return jnp.concatenate([first[:, None], second[:, None]], 1).reshape(-1, width)


def both(core, mine, other):
    return jnp.concatenate(
        [jnp.where(core == 0, mine, other), jnp.where(core == 0, other, mine)], 0
    )


def plain(matrix, panel):
    core = lax.axis_index("col")
    height, width = panel.shape
    half = height // 2
    panel_half = lax.dynamic_slice_in_dim(panel, core * half, half, 0)
    panel_halves = gather(panel_half)
    flat = panel_halves.reshape(-1, width)
    gram = dot(flat, flat, ((0,), (0,)))
    gram = gram + swap(gram)
    panel_cols = columns(panel_halves, core)
    terms = dot(matrix, panel_cols, precision=THREE)
    mine = lax.dynamic_slice_in_dim(terms, core * half, half, 0)
    other = lax.dynamic_slice_in_dim(terms, (1 - core) * half, half, 0)
    image_half = mine + swap(other)
    image_halves = gather(image_half)

    lower = lax.linalg.cholesky(gram, symmetrize_input=False)
    inverse = lax.linalg.triangular_solve(
        lower, jnp.eye(width, dtype=jnp.float32), left_side=True, lower=True
    )
    basis = dot(panel, inverse, ((1,), (1,)))
    left = dot(2.0 * basis, inverse)
    image = both(core, image_half, swap(image_half))
    image = dot(image, inverse, ((1,), (1,)))

    flat_image = image_halves.reshape(-1, width)
    inner = dot(flat, flat_image, ((0,), (0,)))
    inner = inner + swap(inner)
    image_cols = columns(image_halves, core)
    coupling = dot(dot(inverse, inner), inverse, ((1,), (1,)))
    right = dot(2.0 * image - 4.0 * dot(basis, coupling), inverse)
    updated = matrix - dot(
        jnp.concatenate([left, right], 1),
        jnp.concatenate([image_cols, panel_cols], 1),
        ((1,), (1,)),
        THREE,
    )
    return (updated, basis)


AXES = ("row", "col")
COUNT = len(WALK)


def flat(place, core):
    return WALK[place % COUNT] * 2 + core


ROUND = tuple((flat(i, 0), flat(i + 1, 0)) for i in range(COUNT)) + tuple(
    (flat(i, 1), flat(i - 1, 1)) for i in range(COUNT)
)


def order_table():
    table = np.zeros((COUNT, 2, 4, 2), np.int32)
    for row in range(COUNT):
        place = WALK.index(row)
        for core in range(2):
            away = -1 if core == 0 else 1
            found = []
            for piece in range(COUNT):
                step, first = (piece + 1) // 2, piece % 2 == 1
                origin = WALK[(place + (away if first else -away) * step) % COUNT]
                if origin // 4 == core:
                    found.append((step, piece, origin % 4))
            found.sort()
            for k, (_, piece, block) in enumerate(found):
                table[row, core, k] = piece, block
    return table.reshape(COUNT * 2, 8)


def entry(table, k):
    device = lax.axis_index("row") * 2 + lax.axis_index("col")
    return table[device, 2 * k], table[device, 2 * k + 1]


def split(x):
    high = x.astype(jnp.bfloat16)
    return high, (x - high.astype(jnp.float32)).astype(jnp.bfloat16)


def dot3(a, b, dims=((1,), (0,))):
    one = lambda x, y: lax.dot_general(
        x, y, (dims, ((), ())), preferred_element_type=jnp.float32
    )
    if dims == ACROSS:
        left = jnp.concatenate([a[0], a[0], a[1]], 1)
        return one(left, jnp.concatenate([b[0], b[1], b[0]], 1))
    return one(a[0], b[0]) + (one(a[0], b[1]) + one(a[1], b[0]))


TURNED = ((0,), (0,))
ACROSS = ((1,), (1,))


def wide(pieces):
    return jnp.concatenate([x[...] for x in pieces], 1)


def cost(flops, bytes_accessed):
    return pl.CostEstimate(
        flops=int(flops), bytes_accessed=int(bytes_accessed), transcendentals=0
    )


def vmem():
    return pl.BlockSpec(memory_space=pltpu.VMEM)


def anywhere():
    return pl.BlockSpec(memory_space=pl.ANY)


def in_hbm():
    return pl.BlockSpec(memory_space=pltpu.HBM)


def in_smem():
    return pl.BlockSpec(memory_space=pltpu.SMEM)


def block_fetch(matrix, table, k, land, sem, parts=6):
    height, width = land.shape
    at = pl.multiple_of(entry(table, k)[1] * width, width)
    step = height // parts
    for low in range(0, height, step):
        pltpu.make_async_copy(
            matrix.at[pl.ds(low, step), pl.ds(at, width)],
            land.at[pl.ds(low, step)],
            sem,
        ).start()


def params(mib):
    return pltpu.CompilerParams(vmem_limit_bytes=mib * 1024 * 1024)


def in_order(one, two):
    first = lax.axis_index("col") == 0
    one, two = one[...], two[...]
    return jnp.concatenate([jnp.where(first, one, two), jnp.where(first, two, one)], 1)


def inner_kernel(start, count, last, *refs):
    total, pieces, out = refs[:start], refs[start:-1], refs[-1]
    acc = total[0][...] if start else None
    lefts, rights = pieces[:count], pieces[count:]
    for i in range(0, count, 2):
        join = in_order if last and i == count - 2 else lambda *x: wide(x)
        left = join(*lefts[i : i + 2])
        right = join(*rights[i : i + 2]) if rights else left
        if rights:
            term = dot3(split(left), split(right), TURNED)
        else:
            term = dot(left, right, TURNED)
        acc = term if acc is None else acc + term
    out[...] = acc


def inner(total, lefts, rights=(), last=False):
    lefts = [x for pair in lefts for x in pair]
    rights = [x for pair in rights for x in pair]
    width = 2 * lefts[0].shape[1]
    rows = sum(x.shape[0] for x in lefts[::2])
    args = ([] if total is None else [total]) + lefts + rights
    return pl.pallas_call(
        functools.partial(
            inner_kernel, 0 if total is None else 1, len(lefts), last
        ),
        out_shape=jax.ShapeDtypeStruct((width, width), jnp.float32),
        in_specs=[vmem()] * len(args),
        out_specs=vmem(),
        compiler_params=params(6),
        cost_estimate=cost(12 * rows * width * width, 8 * rows * width),
    )(*args)


def fetch(pieces, which, lands, sems):
    core = lax.axis_index("col")
    for index, pair in enumerate(pieces):
        turns = ((0, 1), (1, 0)) if index == COUNT - 1 else ((0, 1),)
        for turn, sides in enumerate(turns):
            here = which == index
            if len(turns) > 1:
                here = jnp.logical_and(here, core == turn)

            @pl.when(here)
            def _():
                for source, side in enumerate(sides):
                    pltpu.make_async_copy(
                        pair[source], lands[side], sems.at[side]
                    ).start()


def pick(pieces, which, land):
    for index, pair in enumerate(pieces):
        join = in_order if index == COUNT - 1 else lambda *x: wide(x)

        @pl.when(which == index)
        def _():
            land[...] = join(*pair)


def landed(lands, sems):
    for side in range(2):
        pltpu.make_async_copy(lands[side], lands[side], sems.at[side]).wait()


def pair_up(refs):
    return [refs[i : i + 2] for i in range(0, len(refs), 2)]


def load_kernel(first, table, matrix, *refs):
    *outs, sems = refs
    for k, out in enumerate(outs):
        block_fetch(matrix, table, first + k, out, sems.at[k])
    for k, out in enumerate(outs):
        pltpu.make_async_copy(out, out, sems.at[k]).wait()


def load(table, matrix, first, blocks):
    height = matrix.shape[0]
    columns = blocks * height
    return pl.pallas_call(
        functools.partial(load_kernel, first),
        in_specs=[in_smem(), in_hbm()],
        out_specs=[vmem()] * blocks,
        out_shape=[jax.ShapeDtypeStruct((height, height), jnp.float32)] * blocks,
        scratch_shapes=[pltpu.SemaphoreType.DMA((blocks,))],
        compiler_params=params(46),
        cost_estimate=cost(height * columns, 8 * height * columns),
    )(table, matrix)


def term_kernel(first, blocks, count, *refs):
    table, matrix, refs = refs[0], refs[1 : 1 + blocks], refs[1 + blocks :]
    start = 2 if first else 0
    total, refs = refs[:start], refs[start:]
    pieces = pair_up(refs[:count])
    out0, out1, kept_high, kept_low, land = refs[count:]
    height, middle = out0.shape
    acc = wide(total) if start else None
    for k in range(blocks):
        left = split(matrix[k][...])
        pick(pieces, entry(table, first + k)[0], land)
        right = split(land[...])
        rows = slice(k * height, k * height + height)
        kept_high[rows], kept_low[rows] = right
        term = dot3(left, right)
        acc = term if acc is None else acc + term
    out0[...], out1[...] = acc[:, :middle], acc[:, middle:]


def terms(table, matrix, total, pieces, first):
    blocks, height = len(matrix), matrix[0].shape[0]
    middle = pieces[0][0].shape[1]
    width = 2 * middle
    flat_pieces = [x for pair in pieces for x in pair]
    begin = [] if total is None else list(total)
    *total, high, low = pl.pallas_call(
        functools.partial(term_kernel, first, blocks, len(flat_pieces)),
        in_specs=[in_smem()]
        + [vmem()] * (blocks + len(begin) + len(flat_pieces)),
        out_specs=[vmem()] * 4,
        scratch_shapes=[pltpu.VMEM((height, width), jnp.float32)],
        out_shape=[jax.ShapeDtypeStruct((height, middle), jnp.float32)] * 2
        + [jax.ShapeDtypeStruct((blocks * height, width), jnp.bfloat16)] * 2,
        compiler_params=params(11),
        cost_estimate=cost(
            6 * blocks * height * height * width, 4 * blocks * height * height
        ),
    )(table, *matrix, *begin, *flat_pieces)
    return total, (high, low)


def factor(out, work, rows, tops, block=64, group=8):
    size = out.shape[0]
    index = lax.broadcasted_iota(jnp.int32, (block, 128), 0)
    for top in tops:
        low = top // 128 * 128
        high = low + 128
        strip = jnp.concatenate(
            [work[top : top + block, low:], rows[top : top + block, :high]], 1
        )
        tiles = strip.shape[1] // 128
        spread = lambda x: jnp.concatenate([x] * tiles, 1)
        pivots = jnp.ones((block, 128), jnp.float32)
        for j in range(0, block, group):
            at = top - low + j
            some = range(group)
            down = [
                jnp.broadcast_to(strip[:, at + m : at + m + 1], (block, 128))
                for m in some
            ]
            along = [strip[j + m : j + m + 1, :] for m in some]
            cell = {
                (m, i): jnp.broadcast_to(
                    strip[j + m : j + m + 1, at + i : at + i + 1], (1, 128)
                )
                for m in some
                for i in range(m, group)
            }
            for m in some:
                over = 1.0 / cell[m, m]
                pivots = jnp.where(index == j + m, cell[m, m], pivots)
                row = along[m] * spread(over)
                strip = strip - spread(jnp.where(index > j + m, down[m], 0.0)) * row
                for i in range(m + 1, group):
                    ratio = cell[m, i] * over
                    along[i] = along[i] - spread(cell[m, i]) * row
                    down[i] = down[i] - down[m] * ratio
                    for h in range(i, group):
                        cell[i, h] = cell[i, h] - cell[m, h] * ratio
        strip = strip * spread(lax.rsqrt(pivots))
        out[top : top + block, :high] = strip[:, size - low :]
        if high < size:
            out[top : top + block, high:] = jnp.zeros(
                (block, size - high), jnp.float32
            )
        after = top + block
        if after < size:
            base = after // 128 * 128
            update = dot(strip[:, base - low : size - low], strip[:, base - low :], TURNED)
            update = update[after - base :]
            work[after:, base:] -= update[:, : size - base]
            rows[after:, :high] -= update[:, size - base :]


def first_kernel(gram, out, work, rows):
    size = gram.shape[0]
    work[...] = gram[...]
    line = lax.broadcasted_iota(jnp.int32, (size, size), 0)
    lane = lax.broadcasted_iota(jnp.int32, (size, size), 1)
    rows[...] = jnp.where(line == lane, 1.0, 0.0).astype(jnp.float32)
    factor(out, work, rows, range(0, size // 2, 64))
    out[size // 2 :, :] = jnp.zeros((size // 2, size), jnp.float32)


def second_kernel(begun, work_in, rows_in, out, work, rows):
    size = out.shape[0]
    work[...] = work_in[...]
    rows[...] = rows_in[...]
    out[...] = begun[...]
    factor(out, work, rows, range(size // 2, size, 64))


def factor_call(kernel, args, scratch):
    size = args[0].shape[0]
    shape = (size, size)
    outs = 1 if scratch else 3
    return pl.pallas_call(
        kernel,
        out_shape=[jax.ShapeDtypeStruct(shape, jnp.float32)] * outs,
        in_specs=[vmem()] * len(args),
        out_specs=[vmem()] * outs,
        scratch_shapes=[pltpu.VMEM(shape, jnp.float32)] * scratch,
        compiler_params=params(4),
        cost_estimate=cost(4e9, 4 * size * size),
    )(*args)


def left_kernel(panel, image0, image1, inverse, basis, left, right, normal):
    inv = inverse[...]
    rows = dot(panel[...], inv, ACROSS)
    basis[...] = rows
    normal[...] = dot(4.0 * inv, inv, TURNED)
    inv = split(inv)
    left[...] = dot3(split(2.0 * rows), inv)
    image = dot3(split(wide((image0, image1))), inv, ACROSS)
    right[...] = dot3(split(2.0 * image), inv)


def lefts(panel, images, inverse):
    height, width = panel.shape
    return pl.pallas_call(
        left_kernel,
        out_shape=[jax.ShapeDtypeStruct((height, width), jnp.float32)] * 3
        + [jax.ShapeDtypeStruct((width, width), jnp.float32)],
        in_specs=[vmem()] * 4,
        out_specs=[vmem()] * 4,
        compiler_params=params(8),
        cost_estimate=cost(48 * height * width * width, 20 * height * width),
    )(panel, *images, inverse)


def before_kernel(blocks, count, *refs):
    table, left, matrix, refs = refs[0], refs[1], refs[2 : 2 + blocks], refs[2 + blocks :]
    pieces, (out, land) = pair_up(refs[:count]), refs[count:]
    one = split(left[...])
    for k in range(blocks):
        pick(pieces, entry(table, k)[0], land)
        right = split(land[...])
        out[k] = matrix[k][...] - dot3(one, right, ACROSS)


def before(table, matrix, left, pieces):
    blocks = len(matrix)
    height, width = left.shape
    flat_pieces = [x for pair in pieces for x in pair]
    return pl.pallas_call(
        functools.partial(before_kernel, blocks, len(flat_pieces)),
        in_specs=[in_smem()] + [vmem()] * (1 + blocks + len(flat_pieces)),
        out_specs=vmem(),
        scratch_shapes=[pltpu.VMEM((height, width), jnp.float32)],
        out_shape=jax.ShapeDtypeStruct((blocks, height, height), jnp.float32),
        compiler_params=params(10),
        cost_estimate=cost(
            6 * blocks * height * height * width, 8 * blocks * height * height
        ),
    )(table, left, *matrix, *flat_pieces)


def update_kernel(last, *refs):
    table, matrix, early, total, inverse, normal, basis, left, right = refs[:9]
    kept, pieces = pair_up(refs[9:15]), pair_up(refs[15:31])
    panel_last, image_last = refs[31:33], pieces[-1]
    out, held, third, land, out_sems = refs[33:]
    height = left.shape[0]
    pick(pieces, entry(table, last)[0], land)
    acc = total[...] + dot3(
        split(in_order(*panel_last)), split(in_order(*image_last)), TURNED
    )
    middle = dot(inverse[...], dot(acc, normal[...]))
    y = right[...] - dot3(split(basis[...]), split(middle))
    y = split(y)
    third[...] = matrix[...] - dot3(
        split(left[...]), split(land[...]), ACROSS
    )
    slots, width, count = held.shape[0], held.shape[2], 0
    writes = []
    for k in range(last + 1):
        high, low = kept[min(k, 1) if k < last else 2]
        top = 0 if k in (0, last) else (k - 1) * height
        at = entry(table, k)[1] * height
        for low_column in range(0, height, width):
            rows = slice(top + low_column, top + low_column + width)
            columns = slice(low_column, low_column + width)
            term = dot3(y, (high[rows], low[rows]), ACROSS)
            begin = early[k, :, columns] if k < last else third[:, columns]
            slot = count % slots
            if count >= slots:
                writes[count - slots].wait()
            held[slot] = begin - term
            where = pl.ds(pl.multiple_of(at + low_column, width), width)
            writes.append(
                pltpu.make_async_copy(held.at[slot], out.at[:, where], out_sems.at[slot])
            )
            writes[-1].start()
            count += 1
    for write in writes[-slots:]:
        write.wait()


def update(table, matrix, early, total, inverse, normal, basis, left, right, kept, pieces, opposite):
    height, width = basis.shape
    blocks = early.shape[0] + 1
    columns = blocks * height
    flat_pieces = [x for pair in pieces for x in pair]
    return pl.pallas_call(
        functools.partial(update_kernel, blocks - 1),
        in_specs=[in_smem()]
        + [vmem()] * (16 + len(flat_pieces)),
        out_specs=in_hbm(),
        scratch_shapes=[
            pltpu.VMEM((4, height, height // 2), jnp.float32),
            pltpu.VMEM((height, height), jnp.float32),
            pltpu.VMEM((height, width), jnp.float32),
            pltpu.SemaphoreType.DMA((4,)),
        ],
        out_shape=jax.ShapeDtypeStruct((height, columns), jnp.float32),
        compiler_params=params(18),
        cost_estimate=cost(12 * height * columns * width, 8 * height * columns),
    )(
        table, matrix, early, total, inverse, normal, basis, left, right,
        *(x for pair in kept for x in pair),
        *flat_pieces, *opposite,
    )


def hop(x):
    return lax.ppermute(x, AXES, ROUND)


def swapped(pair):
    return tuple(swap(x) for x in pair)


def after(x, *others):
    return lax.optimization_barrier((x, *others))[0]


def ring(matrix, panel):
    panel, first = lax.optimization_barrier((panel, lax.axis_index("col") == 0))
    table = jnp.asarray(order_table())
    middle = panel.shape[1] // 2

    own = (panel[:, :middle], panel[:, middle:])
    early_blocks = load(table, matrix, 0, 2)
    late_blocks = load(table, matrix, 2, 2)
    matrix = (*early_blocks, *late_blocks)
    a1 = (hop(own[0]), hop(own[1]))
    b1 = (swap(after(a1[0], *early_blocks)), swap(a1[1]))
    gram = inner(None, [own, a1, b1])
    a2 = (hop(a1[0]), hop(a1[1]))
    b2 = swapped(a2)
    a3 = (hop(after(a2[0], gram)), hop(a2[1]))
    b3 = swapped(a3)
    gram = inner(gram, [a2, b2])
    image, kept = terms(table, [after(matrix[0], *late_blocks)], None, [own, a1, b1, a2, b2], 0)
    kepts = [kept]
    one = hop(jnp.where(first, a3[0], after(a3[1], image[0])))
    panels = [own, a1, b1, a2, b2, a3, b3]
    image, kept = terms(table, matrix[1:3], image, panels, 1)
    kepts.append(kept)
    opposite = (one, swap(after(one, image[0])))
    image, kept = terms(table, [after(matrix[3], gram)], image, [*panels, opposite], 3)
    kepts.append(kept)

    image = tuple(x + swap(x) for x in image)
    gram = inner(gram, [a3, b3, opposite], last=True)
    c1 = (hop(after(image[0], gram)), hop(image[1]))
    d1 = swapped(c1)
    begun = factor_call(first_kernel, [gram], 0)
    c2 = (hop(after(c1[0], begun[0])), hop(c1[1]))
    (inverse,) = factor_call(second_kernel, begun, 2)
    basis, left, right, normal = lefts(panel, image, inverse)
    total = inner(None, panels[:3], [image, c1, d1])
    c3 = (hop(after(c2[0], inverse)), hop(c2[1]))
    d2 = (swap(after(c2[0], left)), swap(after(c2[1], total)))
    d3 = swapped(c3)
    one = hop(jnp.where(first, c3[0], c3[1]))
    images = [image, c1, d1, c2, d2, c3, d3]
    total = inner(total, panels[3:], images[3:])
    early = before(table, matrix[:3], left, images)
    last = (one, swap(after(one, early)))
    updated = update(
        table, matrix[3], early, total, inverse, normal, basis, left, right, kepts,
        [*images, last], opposite,
    )
    return (updated, basis)


def solution(mesh):
    count, cores = mesh.shape["row"], mesh.shape["col"]
    return jax.shard_map(
        ring if (count, cores) == (len(WALK), 2) else plain,
        mesh=mesh,
        in_specs=(P(("grp", "row"), "col"), P(("grp", "row"), None)),
        out_specs=(P(("grp", "row"), "col"), P(("grp", "row"), None)),
        check_vma=False,
    )
```

```python
import functools

import jax
import jax.numpy as jnp
import numpy as np
from jax import lax
from jax.experimental import pallas as pl
from jax.experimental.pallas import tpu as pltpu
from jax.sharding import PartitionSpec as P

WALK = (0, 2, 4, 6, 7, 5, 3, 1)
FULL = lax.Precision.HIGHEST
THREE = lax.Precision.HIGH


def dot(a, b, dims=((1,), (0,)), precision=FULL):
    return lax.dot_general(
        a, b, (dims, ((), ())), precision=precision, preferred_element_type=jnp.float32
    )


def swap(x):
    return lax.ppermute(x, "col", ((0, 1), (1, 0)))


def gather(part):
    return lax.all_gather(part, "row", axis=0)


def columns(halves, core):
    count, height, width = halves.shape
    mine = lax.dynamic_slice_in_dim(halves, core * (count // 2), count // 2, 0)
    other = lax.dynamic_slice_in_dim(halves, (1 - core) * (count // 2), count // 2, 0)
    other = swap(other)
    first = jnp.where(core == 0, mine, other)
    second = jnp.where(core == 0, other, mine)
    return jnp.concatenate([first[:, None], second[:, None]], 1).reshape(-1, width)


def both(core, mine, other):
    return jnp.concatenate(
        [jnp.where(core == 0, mine, other), jnp.where(core == 0, other, mine)], 0
    )


def plain(matrix, panel):
    core = lax.axis_index("col")
    height, width = panel.shape
    half = height // 2
    panel_half = lax.dynamic_slice_in_dim(panel, core * half, half, 0)
    panel_halves = gather(panel_half)
    flat = panel_halves.reshape(-1, width)
    gram = dot(flat, flat, ((0,), (0,)))
    gram = gram + swap(gram)
    panel_cols = columns(panel_halves, core)
    terms = dot(matrix, panel_cols, precision=THREE)
    mine = lax.dynamic_slice_in_dim(terms, core * half, half, 0)
    other = lax.dynamic_slice_in_dim(terms, (1 - core) * half, half, 0)
    image_half = mine + swap(other)
    image_halves = gather(image_half)

    lower = lax.linalg.cholesky(gram, symmetrize_input=False)
    inverse = lax.linalg.triangular_solve(
        lower, jnp.eye(width, dtype=jnp.float32), left_side=True, lower=True
    )
    basis = dot(panel, inverse, ((1,), (1,)))
    left = dot(2.0 * basis, inverse)
    image = both(core, image_half, swap(image_half))
    image = dot(image, inverse, ((1,), (1,)))

    flat_image = image_halves.reshape(-1, width)
    inner = dot(flat, flat_image, ((0,), (0,)))
    inner = inner + swap(inner)
    image_cols = columns(image_halves, core)
    coupling = dot(dot(inverse, inner), inverse, ((1,), (1,)))
    right = dot(2.0 * image - 4.0 * dot(basis, coupling), inverse)
    updated = matrix - dot(
        jnp.concatenate([left, right], 1),
        jnp.concatenate([image_cols, panel_cols], 1),
        ((1,), (1,)),
        THREE,
    )
    return (updated, basis)


AXES = ("row", "col")
COUNT = len(WALK)


def flat(place, core):
    return WALK[place % COUNT] * 2 + core


ROUND = tuple((flat(i, 0), flat(i + 1, 0)) for i in range(COUNT)) + tuple(
    (flat(i, 1), flat(i - 1, 1)) for i in range(COUNT)
)


def order_table():
    table = np.zeros((COUNT, 2, 4, 2), np.int32)
    for row in range(COUNT):
        place = WALK.index(row)
        for core in range(2):
            away = -1 if core == 0 else 1
            found = []
            for piece in range(COUNT):
                step, first = (piece + 1) // 2, piece % 2 == 1
                origin = WALK[(place + (away if first else -away) * step) % COUNT]
                if origin // 4 == core:
                    found.append((step, piece, origin % 4))
            found.sort()
            for k, (_, piece, block) in enumerate(found):
                table[row, core, k] = piece, block
    return table.reshape(COUNT * 2, 8)


def entry(table, k):
    device = lax.axis_index("row") * 2 + lax.axis_index("col")
    return table[device, 2 * k], table[device, 2 * k + 1]


def split(x):
    high = x.astype(jnp.bfloat16)
    return high, (x - high.astype(jnp.float32)).astype(jnp.bfloat16)


def dot3(a, b, dims=((1,), (0,))):
    one = lambda x, y: lax.dot_general(
        x, y, (dims, ((), ())), preferred_element_type=jnp.float32
    )
    if dims == ACROSS:
        left = jnp.concatenate([a[0], a[0], a[1]], 1)
        return one(left, jnp.concatenate([b[0], b[1], b[0]], 1))
    if dims != TURNED:
        left = jnp.concatenate([a[0], a[0], a[1]], 1)
        return one(left, jnp.concatenate([b[0], b[1], b[0]], 0))
    return one(a[0], b[0]) + (one(a[0], b[1]) + one(a[1], b[0]))


TURNED = ((0,), (0,))
ACROSS = ((1,), (1,))


def wide(pieces):
    return jnp.concatenate([x[...] for x in pieces], 1)


def cost(flops, bytes_accessed):
    return pl.CostEstimate(
        flops=int(flops), bytes_accessed=int(bytes_accessed), transcendentals=0
    )


def vmem():
    return pl.BlockSpec(memory_space=pltpu.VMEM)


def anywhere():
    return pl.BlockSpec(memory_space=pl.ANY)


def in_hbm():
    return pl.BlockSpec(memory_space=pltpu.HBM)


def in_smem():
    return pl.BlockSpec(memory_space=pltpu.SMEM)


def block_fetch(matrix, table, k, land, sem, parts=6):
    height, width = land.shape
    at = pl.multiple_of(entry(table, k)[1] * width, width)
    step = height // parts
    for low in range(0, height, step):
        pltpu.make_async_copy(
            matrix.at[pl.ds(low, step), pl.ds(at, width)],
            land.at[pl.ds(low, step)],
            sem,
        ).start()


def params(mib):
    return pltpu.CompilerParams(vmem_limit_bytes=mib * 1024 * 1024)


def in_order(one, two):
    first = lax.axis_index("col") == 0
    one, two = one[...], two[...]
    return jnp.concatenate([jnp.where(first, one, two), jnp.where(first, two, one)], 1)


def inner_kernel(start, count, last, *refs):
    total, pieces, out = refs[:start], refs[start:-1], refs[-1]
    acc = total[0][...] if start else None
    lefts, rights = pieces[:count], pieces[count:]
    for i in range(0, count, 2):
        join = in_order if last and i == count - 2 else lambda *x: wide(x)
        left = join(*lefts[i : i + 2])
        right = join(*rights[i : i + 2]) if rights else left
        if rights:
            term = dot3(split(left), split(right), TURNED)
        else:
            term = dot(left, right, TURNED)
        acc = term if acc is None else acc + term
    out[...] = acc


def inner(total, lefts, rights=(), last=False):
    lefts = [x for pair in lefts for x in pair]
    rights = [x for pair in rights for x in pair]
    width = 2 * lefts[0].shape[1]
    rows = sum(x.shape[0] for x in lefts[::2])
    args = ([] if total is None else [total]) + lefts + rights
    return pl.pallas_call(
        functools.partial(
            inner_kernel, 0 if total is None else 1, len(lefts), last
        ),
        out_shape=jax.ShapeDtypeStruct((width, width), jnp.float32),
        in_specs=[vmem()] * len(args),
        out_specs=vmem(),
        compiler_params=params(6),
        cost_estimate=cost(12 * rows * width * width, 8 * rows * width),
    )(*args)


def fetch(pieces, which, lands, sems):
    core = lax.axis_index("col")
    for index, pair in enumerate(pieces):
        turns = ((0, 1), (1, 0)) if index == COUNT - 1 else ((0, 1),)
        for turn, sides in enumerate(turns):
            here = which == index
            if len(turns) > 1:
                here = jnp.logical_and(here, core == turn)

            @pl.when(here)
            def _():
                for source, side in enumerate(sides):
                    pltpu.make_async_copy(
                        pair[source], lands[side], sems.at[side]
                    ).start()


def pick(pieces, which, land):
    for index, pair in enumerate(pieces):
        join = in_order if index == COUNT - 1 else lambda *x: wide(x)

        @pl.when(which == index)
        def _():
            land[...] = join(*pair)


def landed(lands, sems):
    for side in range(2):
        pltpu.make_async_copy(lands[side], lands[side], sems.at[side]).wait()


def pair_up(refs):
    return [refs[i : i + 2] for i in range(0, len(refs), 2)]


def load_kernel(first, table, matrix, *refs):
    *outs, sems = refs
    for k, out in enumerate(outs):
        block_fetch(matrix, table, first + k, out, sems.at[k])
    for k, out in enumerate(outs):
        pltpu.make_async_copy(out, out, sems.at[k]).wait()


def load(table, matrix, first, blocks):
    height = matrix.shape[0]
    columns = blocks * height
    return pl.pallas_call(
        functools.partial(load_kernel, first),
        in_specs=[in_smem(), in_hbm()],
        out_specs=[vmem()] * blocks,
        out_shape=[jax.ShapeDtypeStruct((height, height), jnp.float32)] * blocks,
        scratch_shapes=[pltpu.SemaphoreType.DMA((blocks,))],
        compiler_params=params(46),
        cost_estimate=cost(height * columns, 8 * height * columns),
    )(table, matrix)


def term_kernel(first, blocks, count, *refs):
    table, matrix, refs = refs[0], refs[1 : 1 + blocks], refs[1 + blocks :]
    start = 2 if first else 0
    total, refs = refs[:start], refs[start:]
    pieces = pair_up(refs[:count])
    out0, out1, kept_high, kept_low, land = refs[count:]
    height, middle = out0.shape
    acc = wide(total) if start else None
    for k in range(blocks):
        left = split(matrix[k][...])
        pick(pieces, entry(table, first + k)[0], land)
        right = split(land[...])
        rows = slice(k * height, k * height + height)
        kept_high[rows], kept_low[rows] = right
        term = dot3(left, right)
        acc = term if acc is None else acc + term
    out0[...], out1[...] = acc[:, :middle], acc[:, middle:]


def terms(table, matrix, total, pieces, first):
    blocks, height = len(matrix), matrix[0].shape[0]
    middle = pieces[0][0].shape[1]
    width = 2 * middle
    flat_pieces = [x for pair in pieces for x in pair]
    begin = [] if total is None else list(total)
    *total, high, low = pl.pallas_call(
        functools.partial(term_kernel, first, blocks, len(flat_pieces)),
        in_specs=[in_smem()]
        + [vmem()] * (blocks + len(begin) + len(flat_pieces)),
        out_specs=[vmem()] * 4,
        scratch_shapes=[pltpu.VMEM((height, width), jnp.float32)],
        out_shape=[jax.ShapeDtypeStruct((height, middle), jnp.float32)] * 2
        + [jax.ShapeDtypeStruct((blocks * height, width), jnp.bfloat16)] * 2,
        compiler_params=params(17),
        cost_estimate=cost(
            6 * blocks * height * height * width, 4 * blocks * height * height
        ),
    )(table, *matrix, *begin, *flat_pieces)
    return total, (high, low)


def factor(out, work, rows, tops, block=64, group=8):
    size = out.shape[0]
    index = lax.broadcasted_iota(jnp.int32, (block, 128), 0)
    for top in tops:
        low = top // 128 * 128
        high = low + 128
        strip = jnp.concatenate(
            [work[top : top + block, low:], rows[top : top + block, :high]], 1
        )
        tiles = strip.shape[1] // 128
        spread = lambda x: jnp.concatenate([x] * tiles, 1)
        pivots = jnp.ones((block, 128), jnp.float32)
        for j in range(0, block, group):
            at = top - low + j
            some = range(group)
            down = [
                jnp.broadcast_to(strip[:, at + m : at + m + 1], (block, 128))
                for m in some
            ]
            along = [strip[j + m : j + m + 1, :] for m in some]
            cell = {
                (m, i): jnp.broadcast_to(
                    strip[j + m : j + m + 1, at + i : at + i + 1], (1, 128)
                )
                for m in some
                for i in range(m, group)
            }
            for m in some:
                over = 1.0 / cell[m, m]
                pivots = jnp.where(index == j + m, cell[m, m], pivots)
                row = along[m] * spread(over)
                strip = strip - spread(jnp.where(index > j + m, down[m], 0.0)) * row
                for i in range(m + 1, group):
                    ratio = cell[m, i] * over
                    along[i] = along[i] - spread(cell[m, i]) * row
                    down[i] = down[i] - down[m] * ratio
                    for h in range(i, group):
                        cell[i, h] = cell[i, h] - cell[m, h] * ratio
        strip = strip * spread(lax.rsqrt(pivots))
        out[top : top + block, :high] = strip[:, size - low :]
        if high < size:
            out[top : top + block, high:] = jnp.zeros(
                (block, size - high), jnp.float32
            )
        after = top + block
        if after < size:
            base = after // 128 * 128
            update = dot(strip[:, base - low : size - low], strip[:, base - low :], TURNED)
            update = update[after - base :]
            work[after:, base:] -= update[:, : size - base]
            rows[after:, :high] -= update[:, size - base :]


def first_kernel(gram, out, work, rows):
    size = gram.shape[0]
    work[...] = gram[...]
    line = lax.broadcasted_iota(jnp.int32, (size, size), 0)
    lane = lax.broadcasted_iota(jnp.int32, (size, size), 1)
    rows[...] = jnp.where(line == lane, 1.0, 0.0).astype(jnp.float32)
    factor(out, work, rows, range(0, size // 2, 64))
    out[size // 2 :, :] = jnp.zeros((size // 2, size), jnp.float32)


def second_kernel(begun, work_in, rows_in, out, work, rows):
    size = out.shape[0]
    work[...] = work_in[...]
    rows[...] = rows_in[...]
    out[...] = begun[...]
    factor(out, work, rows, range(size // 2, size, 64))


def factor_call(kernel, args, scratch):
    size = args[0].shape[0]
    shape = (size, size)
    outs = 1 if scratch else 3
    return pl.pallas_call(
        kernel,
        out_shape=[jax.ShapeDtypeStruct(shape, jnp.float32)] * outs,
        in_specs=[vmem()] * len(args),
        out_specs=[vmem()] * outs,
        scratch_shapes=[pltpu.VMEM(shape, jnp.float32)] * scratch,
        compiler_params=params(4),
        cost_estimate=cost(4e9, 4 * size * size),
    )(*args)


def left_kernel(panel, image0, image1, inverse, basis, left, right, normal):
    inv = inverse[...]
    rows = dot(panel[...], inv, ACROSS)
    basis[...] = rows
    normal[...] = dot(4.0 * inv, inv, TURNED)
    inv = split(inv)
    left[...] = dot3(split(2.0 * rows), inv)
    image = dot3(split(wide((image0, image1))), inv, ACROSS)
    right[...] = dot3(split(2.0 * image), inv)


def lefts(panel, images, inverse):
    height, width = panel.shape
    return pl.pallas_call(
        left_kernel,
        out_shape=[jax.ShapeDtypeStruct((height, width), jnp.float32)] * 3
        + [jax.ShapeDtypeStruct((width, width), jnp.float32)],
        in_specs=[vmem()] * 4,
        out_specs=[vmem()] * 4,
        compiler_params=params(10),
        cost_estimate=cost(48 * height * width * width, 20 * height * width),
    )(panel, *images, inverse)


def before_kernel(blocks, count, *refs):
    table, left, matrix, refs = refs[0], refs[1], refs[2 : 2 + blocks], refs[2 + blocks :]
    pieces, (out, land) = pair_up(refs[:count]), refs[count:]
    one = split(left[...])
    for k in range(blocks):
        pick(pieces, entry(table, k)[0], land)
        right = split(land[...])
        out[k] = matrix[k][...] - dot3(one, right, ACROSS)


def before(table, matrix, left, pieces):
    blocks = len(matrix)
    height, width = left.shape
    flat_pieces = [x for pair in pieces for x in pair]
    return pl.pallas_call(
        functools.partial(before_kernel, blocks, len(flat_pieces)),
        in_specs=[in_smem()] + [vmem()] * (1 + blocks + len(flat_pieces)),
        out_specs=vmem(),
        scratch_shapes=[pltpu.VMEM((height, width), jnp.float32)],
        out_shape=jax.ShapeDtypeStruct((blocks, height, height), jnp.float32),
        compiler_params=params(10),
        cost_estimate=cost(
            6 * blocks * height * height * width, 8 * blocks * height * height
        ),
    )(table, left, *matrix, *flat_pieces)


def update_kernel(last, *refs):
    table, matrix, early, total, inverse, normal, basis, left, right = refs[:9]
    kept, pieces = pair_up(refs[9:15]), pair_up(refs[15:31])
    panel_last, image_last = refs[31:33], pieces[-1]
    out, held, third, land, out_sems = refs[33:]
    height = left.shape[0]
    pick(pieces, entry(table, last)[0], land)
    acc = total[...] + dot3(
        split(in_order(*panel_last)), split(in_order(*image_last)), TURNED
    )
    middle = dot(inverse[...], dot(acc, normal[...]))
    y = right[...] - dot3(split(basis[...]), split(middle))
    y = split(y)
    third[...] = matrix[...] - dot3(
        split(left[...]), split(land[...]), ACROSS
    )
    slots, width, count = held.shape[0], held.shape[2], 0
    writes = []
    for k in range(last + 1):
        high, low = kept[min(k, 1) if k < last else 2]
        top = 0 if k in (0, last) else (k - 1) * height
        at = entry(table, k)[1] * height
        for low_column in range(0, height, width):
            rows = slice(top + low_column, top + low_column + width)
            columns = slice(low_column, low_column + width)
            term = dot3(y, (high[rows], low[rows]), ACROSS)
            begin = early[k, :, columns] if k < last else third[:, columns]
            slot = count % slots
            if count >= slots:
                writes[count - slots].wait()
            held[slot] = begin - term
            where = pl.ds(pl.multiple_of(at + low_column, width), width)
            writes.append(
                pltpu.make_async_copy(held.at[slot], out.at[:, where], out_sems.at[slot])
            )
            writes[-1].start()
            count += 1
    for write in writes[-slots:]:
        write.wait()


def update(table, matrix, early, total, inverse, normal, basis, left, right, kept, pieces, opposite):
    height, width = basis.shape
    blocks = early.shape[0] + 1
    columns = blocks * height
    flat_pieces = [x for pair in pieces for x in pair]
    return pl.pallas_call(
        functools.partial(update_kernel, blocks - 1),
        in_specs=[in_smem()]
        + [vmem()] * (16 + len(flat_pieces)),
        out_specs=in_hbm(),
        scratch_shapes=[
            pltpu.VMEM((4, height, height // 2), jnp.float32),
            pltpu.VMEM((height, height), jnp.float32),
            pltpu.VMEM((height, width), jnp.float32),
            pltpu.SemaphoreType.DMA((4,)),
        ],
        out_shape=jax.ShapeDtypeStruct((height, columns), jnp.float32),
        compiler_params=params(18),
        cost_estimate=cost(12 * height * columns * width, 8 * height * columns),
    )(
        table, matrix, early, total, inverse, normal, basis, left, right,
        *(x for pair in kept for x in pair),
        *flat_pieces, *opposite,
    )


def hop(x):
    return lax.ppermute(x, AXES, ROUND)


def swapped(pair):
    return tuple(swap(x) for x in pair)


def after(x, *others):
    return lax.optimization_barrier((x, *others))[0]


def ring(matrix, panel):
    panel, first = lax.optimization_barrier((panel, lax.axis_index("col") == 0))
    table = jnp.asarray(order_table())
    middle = panel.shape[1] // 2

    own = (panel[:, :middle], panel[:, middle:])
    early_blocks = load(table, matrix, 0, 2)
    late_blocks = load(table, matrix, 2, 2)
    matrix = (*early_blocks, *late_blocks)
    a1 = (hop(own[0]), hop(own[1]))
    b1 = (swap(after(a1[0], *early_blocks)), swap(a1[1]))
    gram = inner(None, [own, a1, b1])
    a2 = (hop(a1[0]), hop(a1[1]))
    b2 = swapped(a2)
    a3 = (hop(after(a2[0], gram)), hop(a2[1]))
    b3 = swapped(a3)
    gram = inner(gram, [a2, b2])
    image, kept = terms(table, [after(matrix[0], *late_blocks)], None, [own, a1, b1, a2, b2], 0)
    kepts = [kept]
    one = hop(jnp.where(first, a3[0], after(a3[1], image[0])))
    panels = [own, a1, b1, a2, b2, a3, b3]
    image, kept = terms(table, matrix[1:3], image, panels, 1)
    kepts.append(kept)
    opposite = (one, swap(after(one, image[0])))
    image, kept = terms(table, [after(matrix[3], gram)], image, [*panels, opposite], 3)
    kepts.append(kept)

    image = tuple(x + swap(x) for x in image)
    gram = inner(gram, [a3, b3, opposite], last=True)
    c1 = (hop(after(image[0], gram)), hop(image[1]))
    d1 = swapped(c1)
    begun = factor_call(first_kernel, [gram], 0)
    c2 = (hop(after(c1[0], begun[0])), hop(c1[1]))
    (inverse,) = factor_call(second_kernel, begun, 2)
    basis, left, right, normal = lefts(panel, image, inverse)
    total = inner(None, panels[:3], [image, c1, d1])
    c3 = (hop(after(c2[0], inverse)), hop(c2[1]))
    d2 = (swap(after(c2[0], left)), swap(after(c2[1], total)))
    d3 = swapped(c3)
    one = hop(jnp.where(first, c3[0], c3[1]))
    images = [image, c1, d1, c2, d2, c3, d3]
    total = inner(total, panels[3:], images[3:])
    early = before(table, matrix[:3], left, images)
    last = (one, swap(after(one, early)))
    updated = update(
        table, matrix[3], early, total, inverse, normal, basis, left, right, kepts,
        [*images, last], opposite,
    )
    return (updated, basis)


def solution(mesh):
    count, cores = mesh.shape["row"], mesh.shape["col"]
    return jax.shard_map(
        ring if (count, cores) == (len(WALK), 2) else plain,
        mesh=mesh,
        in_specs=(P(("grp", "row"), "col"), P(("grp", "row"), None)),
        out_specs=(P(("grp", "row"), "col"), P(("grp", "row"), None)),
        check_vma=False,
    )
```
